128 devices in a mesh: expert: 4 (over z_hi, core), context: 16 (over y, x), dp: 2 (over z_lo).
Axes of the slice: x: 4, y: 4, z: 4 (z_hi: 2, z_lo: 2; z = z_hi * 2 + z_lo), core: 2. Of those that a mesh axis runs over, the one named last changes fastest.
Arguments:
- inputs: bfloat16 [8, 2048, 768], P(('expert', 'dp'), 'context'), may hold values from -6 to 6
- cotangent: bfloat16 [8, 2048, 768], P(('expert', 'dp'), 'context'), may hold values from -6 to 6
- norm1_gain: bfloat16 [768], replicated, may hold values from 0.5 to 1.5
- w_query: bfloat16 [768, 768], replicated, may hold values from -0.21875 to 0.21875
- w_key: bfloat16 [768, 768], replicated, may hold values from -0.21875 to 0.21875
- w_value: bfloat16 [768, 768], replicated, may hold values from -0.21875 to 0.21875
- w_output: bfloat16 [768, 768], replicated, may hold values from -3.5 to 3.5
- bias_table: bfloat16 [32, 12], replicated, may hold values from -4 to 4
- buckets: int32 [4095], replicated, may hold values from 0 to 31
- norm2_gain: bfloat16 [768], replicated, may hold values from 0.5 to 1.5
- w_router: bfloat16 [768, 4], replicated, may hold values from -0.15625 to 0.15625
- routes: int32 [8, 2048, 1], P(('expert', 'dp'), 'context'), may hold values from 0 to 3; in each aligned block of 128 rows (0 to 127, 128 to 255, ..., all dimensions but the last counted through in order) at most 40 rows name the same one
- w_in: bfloat16 [4, 768, 3072], P('expert'), may hold values from -0.21875 to 0.21875
- w_out: bfloat16 [4, 3072, 768], P('expert'), may hold values from -0.4375 to 0.4375
Outputs:
- mixed: bfloat16 [8, 2048, 768], P(('expert', 'dp'), 'context')
- grad_input: bfloat16 [8, 2048, 768], P(('expert', 'dp'), 'context')
- grad_norm1_gain: float32 [768], replicated
- grad_w_query: float32 [768, 768], replicated
- grad_w_key: float32 [768, 768], replicated
- grad_w_value: float32 [768, 768], replicated
- grad_w_output: float32 [768, 768], replicated
- grad_bias_table: float32 [32, 12], replicated
- grad_norm2_gain: float32 [768], replicated
- grad_w_router: float32 [768, 4], replicated
- grad_w_in: float32 [4, 768, 3072], P('expert', None, ('context', 'dp'))
- grad_w_out: float32 [4, 3072, 768], P('expert', ('context', 'dp'))
The draws below stay inside these ranges and needn't reach their ends.
Inputs may be any that keep to these rules, and one draw needn't show every extreme that they name: `routes`: among the 128 rows of one device (aligned blocks of the flattened sequences), no expert is named more than 40 times, and in every draw some expert is named exactly 40 times in some device's rows.
All inputs are finite; a program needn't handle non-finite values.
Results may differ from the reference program's by a relative error of at most 0.025.
Values may be sent and summed in bfloat16 or wider, within the bound.
No kernel may reach another device: no remote copies, remote signals or barrier semaphores. Data moves between devices by JAX's collectives and lax.ppermute only.
A program may use at most 384 MiB of HBM per device.

```python
import math
from functools import partial
import jax
import jax.numpy as jnp
import numpy as np
from jax import lax

D = 768
H = 12
HD = 64
FF = 3072
NBUCKET = 32
SEQ_LEN = 2048
TOK_DEV = 128
SEQS = 8
EXPERTS = 4
CAP = 40


def plant(values, own_key, low, largest):
    longest = values.shape.index(max(values.shape))
    spots = []
    for shift in (0, 1):
        where = [jax.random.randint(jax.random.fold_in(own_key, axis), (), 0, length) for axis, length in enumerate(values.shape)]
        where[longest] = (where[longest] + shift) % values.shape[longest]
        spots.append(tuple(where))
    return values.at[spots[0]].set(low).at[spots[1]].set(largest)


def level_of(stream_key, dims, split, least, high):
    factor_of, own = 1.0, jax.random.fold_in(stream_key, 6)
    for axis_at, blocks in split:
        draws = jnp.exp(jax.random.uniform(jax.random.fold_in(own, axis_at), (blocks,), jnp.float32, least / len(split), high / len(split)))
        factor_of = factor_of * jnp.repeat(draws, dims[axis_at] // blocks).reshape([-1 if axis == axis_at else 1 for axis in range(len(dims))])
    return factor_of


def routed_block(stream_key, own, number, rows, count, top, most, slope):
    ranking = jax.random.permutation(stream_key, count)
    heavy_load, usual = shares(count, rows * top, most, slope, True), shares(count, rows * top, most, slope, False)
    places = jnp.arange(count)

    def named(sizes, rotation):
        used = int((sizes > 0).sum())
        fixed = max(1, used // 4)
        passed = fixed + (places - fixed + rotation * (used - fixed)) % max(1, count - fixed)
        return jnp.zeros((count,), jnp.int32).at[ranking[jnp.where(places < fixed, places, passed)]].set(jnp.asarray(sizes, jnp.int32))

    sizes = jnp.where(number % 4 == 0, named(heavy_load, number // 4), named(usual, number - number // 4 - 1))
    mixed = jax.random.permutation(jax.random.fold_in(own, 3), count)
    giver, sink = mixed[0:count // 2 * 2:2], mixed[1:count // 2 * 2:2]
    margin = jnp.minimum(sizes[giver] - 1, most - sizes[sink]) // 2
    margin = jnp.where((giver == ranking[0]) | (sink == ranking[0]) | (sizes[sink] == 0), 0, jnp.maximum(margin, 0))
    passed = jax.random.randint(jax.random.fold_in(own, 4), (count // 2,), 0, 1 << 20) % (margin + 1)
    sizes = sizes.at[giver].add(-passed).at[sink].add(passed)
    members = jnp.searchsorted(jnp.cumsum(sizes), jnp.arange(rows * top), side="right").astype(jnp.int32)
    grid = members.reshape(top, rows).T
    grid = grid[jax.random.permutation(jax.random.fold_in(own, 1), rows)]
    rotation = jax.random.randint(jax.random.fold_in(own, 2), (rows, 1), 0, top)
    return jnp.take_along_axis(grid, (jnp.arange(top)[None, :] + rotation) % top, axis=1)


def shares(number_of, total, most, slope, full):
    loads = [(1 << 20) // math.isqrt(grade ** slope) + 1 for grade in range(1, number_of + 1)]
    largest = most if full else min(most, max(-(-total // number_of), total * loads[0] // sum(loads)))
    least = 1 if total - largest >= number_of - 1 else 0
    holding, surplus = [largest] + [least] * (number_of - 1), total - largest - least * (number_of - 1)
    while surplus > 0:
        free = [i for i in range(1, number_of) if holding[i] < largest] or [i for i in range(1, number_of) if holding[i] < most]
        mass, budget = sum([loads[i] for i in free]), surplus
        for i in free:
            addition = min(most - holding[i], max(1, budget * loads[i] // mass), surplus)
            holding[i] = holding[i] + addition
            surplus = surplus - addition
    return np.array(holding)


def centred(key, dims, spread, bound, shards=(), kind=jnp.bfloat16):
    values = spread * jax.random.normal(key, dims, jnp.float32)
    if shards:
        values = values * level_of(key, dims, shards, -0.22, 0.18)
    return jnp.clip(values, -bound, bound).astype(kind)


def setup_inputs(seed: int = 0) -> dict:
    streams_of = jax.random.split(jax.random.key(seed), 15)
    inputs = centred(streams_of[0], (SEQS, SEQ_LEN, D), 1.0, 6.0, ((0, 8), (1, 16)))
    cotangent = centred(streams_of[1], (SEQS, SEQ_LEN, D), 1.0, 6.0, ((0, 8), (1, 16)))
    norm1_gain = jnp.clip(1.0 + 0.1 * jax.random.normal(streams_of[2], (D,), jnp.float32), 0.5, 1.5).astype(jnp.bfloat16)
    w_query = centred(streams_of[3], (D, D), D ** -0.5, 0.21875)
    w_key = centred(streams_of[4], (D, D), D ** -0.5, 0.21875)
    w_value = centred(streams_of[5], (D, D), D ** -0.5, 0.21875)
    w_output = centred(streams_of[6], (D, D), (max(D // 256, 1)) ** -0.5, 3.5)
    bias_table = centred(streams_of[7], (NBUCKET, H), 1.0, 4.0)
    buckets = plant(jax.random.randint(streams_of[8], (2 * SEQ_LEN - 1,), 0, NBUCKET), jax.random.fold_in(streams_of[8], 1), 0, NBUCKET - 1).astype(jnp.int32)
    norm2_gain = jnp.clip(1.0 + 0.1 * jax.random.normal(streams_of[9], (D,), jnp.float32), 0.5, 1.5).astype(jnp.bfloat16)
    w_router = centred(streams_of[10], (D, EXPERTS), (2 * D) ** -0.5, 0.15625)
    routes_keys = jax.random.split(jax.random.fold_in(streams_of[11], 1), SEQS * SEQ_LEN // TOK_DEV)
    routes_turns = jax.random.permutation(jax.random.fold_in(streams_of[11], 3), SEQS * SEQ_LEN // TOK_DEV)
    routes = jax.vmap(lambda own, number: routed_block(jax.random.fold_in(streams_of[11], 2), own, number, TOK_DEV, EXPERTS, 1, CAP, 0))(routes_keys, routes_turns).reshape((SEQS, SEQ_LEN, 1))
    w_in = centred(streams_of[12], (EXPERTS, D, FF), D ** -0.5, 0.21875, ((0, 4),))
    w_out = centred(streams_of[13], (EXPERTS, FF, D), (FF // 16) ** -0.5, 0.4375, ((0, 4),))
    return {"inputs": inputs, "cotangent": cotangent, "norm1_gain": norm1_gain, "w_query": w_query, "w_key": w_key, "w_value": w_value, "w_output": w_output, "bias_table": bias_table, "buckets": buckets, "norm2_gain": norm2_gain, "w_router": w_router, "routes": routes, "w_in": w_in, "w_out": w_out}


EPS = 1e-06

@jax.custom_vjp
def low(v):
    return lax.optimization_barrier(v.astype(jnp.bfloat16)).astype(jnp.float32)

@jax.custom_vjp
def low_back(v):
    return v

def low_keep(v):
    return (low(v), None)

def low_pass(kept, grad):
    return (grad,)

def back_keep(v):
    return (v, None)

def back_low(kept, grad):
    return (low(grad),)
low.defvjp(low_keep, low_pass)
low_back.defvjp(back_keep, back_low)

def rms_norm(values, gain):
    return values * lax.rsqrt(lax.optimization_barrier(jnp.mean(values * values, axis=-1, keepdims=True)) + EPS) * gain

def matmul(left, right):
    return jnp.dot(left, right, precision=lax.Precision.HIGHEST)

def rounded(values):
    return low_back(low(values))

def softmax_rows(scores):
    shifted = jnp.exp(scores - lax.optimization_barrier(jnp.max(scores, axis=-1, keepdims=True)))
    return shifted / lax.optimization_barrier(jnp.sum(shifted, axis=-1, keepdims=True))

def attend(triple, bias):
    query, key, value = triple
    length = query.shape[0]
    query4 = query.reshape(length, H, HD)
    key4 = key.reshape(length, H, HD)
    value4 = value.reshape(length, H, HD)
    scores = jnp.einsum('ihd,jhd->hij', query4, key4, precision=lax.Precision.HIGHEST) / math.sqrt(HD) + bias
    scores = low_back(scores)
    weights = low(softmax_rows(scores))
    heads_out = jnp.einsum('hij,jhd->ihd', weights, value4, precision=lax.Precision.HIGHEST)
    return heads_out.reshape(length, H * HD)

def reference(inputs, cotangent, norm1_gain, w_query, w_key, w_value, w_output, bias_table, buckets, norm2_gain, w_router, routes, w_in, w_out):
    seq_count, length, width = inputs.shape
    expert_count = w_router.shape[1]
    tok_count = seq_count * length
    block_count = tok_count // TOK_DEV
    route_blocks = routes.reshape(block_count, TOK_DEV).astype(jnp.int32)
    chosen = (route_blocks[:, :, None] == jnp.arange(expert_count, dtype=jnp.int32)).astype(jnp.int32)
    slot_of = lax.optimization_barrier(jnp.sum((jnp.cumsum(chosen, axis=1) - 1) * chosen, axis=-1)).astype(jnp.int32)
    target = (route_blocks * CAP + slot_of).astype(jnp.int32)
    table_index = jnp.full((block_count, expert_count * CAP), TOK_DEV, jnp.int32)
    table_index = table_index.at[jnp.arange(block_count)[:, None], target].set(jnp.broadcast_to(jnp.arange(TOK_DEV, dtype=jnp.int32)[None, :], (block_count, TOK_DEV)))
    chosen_f = chosen.astype(jnp.float32).reshape(seq_count, length, expert_count)
    positions = jnp.arange(length, dtype=jnp.int32)
    offsets = (positions[None, :] - positions[:, None] + length - 1).astype(jnp.int32)
    bucket_grid = buckets[offsets]

    def forward(inputs_f, gain1, wq, wk, wv, wo, table, gain2, wr, win, wout):
        normed1 = rms_norm(inputs_f, gain1)
        act = low(normed1)
        query = rounded(matmul(act, wq))
        key = rounded(matmul(act, wk))
        value = rounded(matmul(act, wv))
        bias = jnp.transpose(table[bucket_grid], (2, 0, 1))
        heads_out = lax.map(jax.checkpoint(partial(attend, bias=bias)), (query, key, value))
        heads_out = rounded(heads_out)
        resid = inputs_f + low_back(matmul(heads_out, wo))
        normed2 = rms_norm(resid, gain2)
        router_probs = softmax_rows(matmul(normed2, wr))
        gate = lax.optimization_barrier(jnp.sum(router_probs * chosen_f, axis=-1))
        sent = rounded(normed2)
        sent_blocks = jnp.concatenate([sent.reshape(block_count, TOK_DEV, width), jnp.zeros((block_count, 1, width), jnp.float32)], axis=1)
        buffer = jnp.take_along_axis(sent_blocks, table_index[:, :, None], axis=1)
        buffer = buffer.reshape(block_count, expert_count, CAP, width).transpose(1, 0, 2, 3)
        buffer = buffer.reshape(expert_count, block_count * CAP, width)
        pre = low_back(jnp.einsum('erd,edf->erf', buffer, win, precision=lax.Precision.HIGHEST))
        hidden = low(jax.nn.gelu(pre))
        expert_out = rounded(jnp.einsum('erf,efd->erd', hidden, wout, precision=lax.Precision.HIGHEST))
        back = expert_out.reshape(expert_count, block_count, CAP, width).transpose(1, 0, 2, 3)
        back = back.reshape(block_count, expert_count * CAP, width)
        picked = jnp.take_along_axis(back, target[:, :, None], axis=1).reshape(seq_count, length, width)
        return resid + gate[..., None] * picked
    floats = [inputs, norm1_gain, w_query, w_key, w_value, w_output, bias_table, norm2_gain, w_router, w_in, w_out]
    floats = [item.astype(jnp.float32) for item in floats]
    result, pullback = jax.vjp(forward, *floats)
    grads = pullback(cotangent.astype(jnp.float32))
    return (result.astype(jnp.bfloat16), grads[0].astype(jnp.bfloat16), grads[1], grads[2], grads[3], grads[4], grads[5], grads[6], grads[7], grads[8], grads[9], grads[10])
```

```python
import functools
import math

import jax
import jax.numpy as jnp
from jax import lax
from jax.experimental import pallas as pl
from jax.experimental.pallas import tpu as pltpu
from jax.sharding import PartitionSpec as P

EPS = 1e-06
F32 = jnp.float32
BF16 = jnp.bfloat16
NN = (((1,), (0,)), ((), ()))
NT = (((1,), (1,)), ((), ()))
HIGHEST = lax.Precision.HIGHEST
MIB = 1 << 20


def mm(left, right, dims=NN):
    return lax.dot_general(left, right, dims, preferred_element_type=F32)


def rms_stats(values):
    return lax.rsqrt(jnp.mean(values * values, axis=-1, keepdims=True) + EPS)


def rms_back(grad, values, scale, gain):
    weighted = grad * gain
    inner = jnp.mean(weighted * values, axis=-1, keepdims=True)
    return scale * weighted - values * (scale * scale * scale * inner)


def gelu_parts(u):
    c = math.sqrt(2.0 / math.pi)
    sq = u * u
    t = jnp.tanh(c * u * (1.0 + 0.044715 * sq))
    half = 0.5 * (1.0 + t)
    slope = half + (0.5 * c) * u * (1.0 - t * t) * (1.0 + (3 * 0.044715) * sq)
    return u * half, slope


def first_half(shape, size):
    return lax.broadcasted_iota(jnp.int32, shape, 1) < size


def split_pair(pair, size):
    first = first_half(pair.shape, size)
    zero = jnp.zeros_like(pair)
    return jnp.concatenate([jnp.where(first, pair, zero), jnp.where(first, zero, pair)], 0)


def join_pair(stacked, size):
    rows = stacked.shape[0] // 2
    return jnp.where(first_half((rows, 2 * size), size), stacked[:rows], stacked[rows:])


def attend_kernel(act_ref, own_ref, wq_ref, wk_ref, wv_ref, win_ref, *refs):
    q_ref, k_ref, v_ref, o_ref, inv_ref, p_ref, s_ref, m_ref, ext_ref = refs[-9:]
    tok = own_ref.shape[0]
    length = act_ref.shape[0]
    wide = win_ref.shape[2]
    lanes = wq_ref.shape[1]
    size = lanes // 2
    query = mm(own_ref[...], wq_ref[...]).astype(BF16)
    query = query.astype(F32) * (1.0 / math.sqrt(size))
    q_ref[...] = query.astype(BF16)
    both = mm(act_ref[...], jnp.concatenate([wk_ref[...], wv_ref[...]], 1)).astype(BF16)
    k_ref[...] = both[:, :lanes]
    v_ref[...] = both[:, lanes:]
    ext_ref[:, :lanes] = both[:, lanes:]
    ext_ref[:, lanes:] = jnp.ones((length, lanes), BF16)
    s_ref[...] = mm(split_pair(query, size).astype(BF16), k_ref[...], NT)
    sub = lax.broadcasted_iota(jnp.int32, (16, wide), 0)

    def first_band(head):
        band = jnp.broadcast_to(win_ref[0, head : head + 1, :], (16, wide))
        band = pltpu.roll(band, wide - (tok - 1), 1)
        for bit in (1, 2, 4, 8):
            band = jnp.where((sub & bit) != 0, pltpu.roll(band, bit, 1), band)
        return band

    def rows_of(head, r):
        return pl.ds(pl.multiple_of(head * tok + r * 16, 16), 16)

    def add_bias(r, bands):
        for head in range(2):
            rows = rows_of(head, r)
            s = s_ref[rows, :] + bands[head][:, :length]
            s_ref[rows, :] = s
            m_ref[rows, :] = jnp.broadcast_to(jnp.max(s, axis=1, keepdims=True), (16, lanes))
        return tuple(pltpu.roll(band, 16, 1) for band in bands)

    def exponents(r, carry):
        for head in range(2):
            rows = rows_of(head, r)
            top = jnp.concatenate([m_ref[rows, :]] * (length // lanes), 1)
            p_ref[0, rows, :] = jnp.exp(s_ref[rows, :] - top).astype(BF16)
        return carry

    lax.fori_loop(0, tok // 16, add_bias, (first_band(0), first_band(1)))
    lax.fori_loop(0, tok // 16, exponents, 0)
    summed = mm(p_ref[0], ext_ref[...])
    inverse = 1.0 / join_pair(summed[:, lanes:], size)
    inv_ref[...] = inverse
    o_ref[...] = join_pair(summed[:, :lanes], size) * inverse


def attend(act_all, act, w_query, w_key, w_value, window, ready):
    length, width = act_all.shape
    tok = act.shape[0]
    pairs, _, wide = window.shape
    lanes = width // pairs
    column = lambda rows: pl.BlockSpec((rows, lanes), lambda p: (0, p))
    whole = lambda rows: pl.BlockSpec((rows, width), lambda p: (0, 0))
    return pl.pallas_call(
        attend_kernel,
        grid=(pairs,),
        in_specs=[
            whole(length), whole(tok), column(width), column(width), column(width),
            pl.BlockSpec((1, 2, wide), lambda p: (p, 0, 0)),
        ] + [pl.BlockSpec(memory_space=pl.ANY)] * len(ready),
        out_specs=[
            column(tok), column(length), column(length), column(tok), column(tok),
            pl.BlockSpec((1, 2 * tok, length), lambda p: (p, 0, 0)),
        ],
        out_shape=[
            jax.ShapeDtypeStruct((tok, width), BF16),
            jax.ShapeDtypeStruct((length, width), BF16),
            jax.ShapeDtypeStruct((length, width), BF16),
            jax.ShapeDtypeStruct((tok, width), F32),
            jax.ShapeDtypeStruct((tok, width), F32),
            jax.ShapeDtypeStruct((pairs, 2 * tok, length), BF16),
        ],
        scratch_shapes=[
            pltpu.VMEM((2 * tok, length), F32),
            pltpu.VMEM((2 * tok, lanes), F32),
            pltpu.VMEM((length, 2 * lanes), BF16),
        ],
        compiler_params=pltpu.CompilerParams(vmem_limit_bytes=56 * MIB),
        cost_estimate=pl.CostEstimate(
            flops=4 * length * width * width + 8 * tok * length * width,
            bytes_accessed=12 * length * width + 4 * pairs * tok * length,
            transcendentals=2 * pairs * tok * length,
        ),
        name="attend",
    )(act_all, act, w_query, w_key, w_value, window, *ready)


def attend_back_kernel(half_ref, p_ref, do_ref, o_ref, q_ref, k_ref, v_ref, act_ref, own_ref,
                       wqt_ref, wkt_ref, wvt_ref, ready_ref,
                       dq_ref, dkv_ref, grad_ref, gain_ref, diag_ref,
                       dp_ref, ds_ref, delta_ref):
    tok = do_ref.shape[0]
    length = act_ref.shape[0]
    lanes = q_ref.shape[1]
    wide = diag_ref.shape[2]
    size = lanes // 2
    pair = pl.program_id(0)
    grad = do_ref[...].astype(F32)
    grads = split_pair(grad, size)
    delta = jnp.sum(split_pair(grad * o_ref[...], size), axis=1, keepdims=True)
    delta_ref[...] = jnp.broadcast_to(delta, delta_ref.shape)
    dp_ref[...] = mm(grads.astype(BF16), v_ref[...], NT)

    def step(r, totals):
        after = []
        for head in range(2):
            rows = pl.ds(pl.multiple_of(head * tok + r * 16, 16), 16)
            less = jnp.concatenate([delta_ref[rows, :]] * (length // lanes), 1)
            d = p_ref[0, rows, :].astype(F32) * (dp_ref[rows, :] - less)
            ds_ref[rows, :] = d.astype(BF16)
            d = jnp.concatenate([d, jnp.zeros((16, wide - length), F32)], 1)
            after.append(pltpu.roll(totals[head], 16, 1) + d)
        return tuple(after)

    empty = jnp.zeros((16, wide), F32)
    totals = lax.fori_loop(0, tok // 16, step, (empty, empty))
    sub = lax.broadcasted_iota(jnp.int32, (16, wide), 0)
    for head in range(2):
        total = totals[head]
        for bit in (1, 2, 4, 8):
            total = jnp.where((sub & bit) == 0, pltpu.roll(total, bit, 1), total)
        diag_ref[0, head : head + 1, :] = jnp.sum(total, axis=0, keepdims=True)
    dq = join_pair(mm(ds_ref[...], k_ref[...]), size) * (1.0 / math.sqrt(size))
    dq_ref[...] = dq.astype(BF16)
    queries = split_pair(q_ref[...].astype(F32), size)
    dk = mm(queries.T.astype(BF16), ds_ref[...]).astype(BF16)
    dv = mm(grads.T.astype(BF16), p_ref[0]).astype(BF16)
    dkv_ref[0] = dk
    dkv_ref[1] = dv
    weights = mm(jnp.concatenate([dk, dv], 0), act_ref[...])
    parts = (mm(dq.T.astype(BF16), own_ref[...]), weights[:lanes], weights[lanes:])
    gain = jnp.zeros((1, act_ref.shape[1]), F32)
    for i, (found, turned) in enumerate(zip(parts, (wqt_ref, wkt_ref, wvt_ref))):
        grad_ref[i] = found.T.astype(BF16)
        gain = gain + jnp.sum(found * turned[...].astype(F32), axis=0, keepdims=True)

    @pl.when(pair == 0)
    def _():
        gain_ref[...] = gain

    @pl.when(pair > 0)
    def _():
        gain_ref[...] += gain


def attend_back(half, probs, grad_heads, heads, query, key, value, act_all, act, turned, ready):
    length, width = act_all.shape
    tok = query.shape[0]
    pairs = probs.shape[0] // 2
    wide = length + tok
    lanes = width // (2 * pairs)
    column = lambda rows: pl.BlockSpec((rows, lanes), lambda p, h: (0, p + h[0] * pairs))
    whole = lambda rows, cols: pl.BlockSpec((rows, cols), lambda p, h: (0, 0))
    row = pl.BlockSpec((lanes, width), lambda p, h: (p + h[0] * pairs, 0))
    return pl.pallas_call(
        attend_back_kernel,
        grid_spec=pltpu.PrefetchScalarGridSpec(
            num_scalar_prefetch=1,
            grid=(pairs,),
            in_specs=[
                pl.BlockSpec((1, 2 * tok, length), lambda p, h: (p + h[0] * pairs, 0, 0)),
                column(tok), column(tok), column(tok), column(length), column(length),
                whole(length, width), whole(tok, width),
                row, row, row, pl.BlockSpec(memory_space=pl.ANY),
            ],
            out_specs=[
                pl.BlockSpec((tok, lanes), lambda p, h: (0, p)),
                pl.BlockSpec((2, lanes, length), lambda p, h: (0, p, 0)),
                pl.BlockSpec((3, width, lanes), lambda p, h: (0, 0, p)),
                pl.BlockSpec((1, width), lambda p, h: (0, 0)),
                pl.BlockSpec((1, 2, wide), lambda p, h: (p, 0, 0)),
            ],
            scratch_shapes=[
                pltpu.VMEM((2 * tok, length), F32),
                pltpu.VMEM((2 * tok, length), BF16),
                pltpu.VMEM((2 * tok, lanes), F32),
            ],
        ),
        out_shape=[
            jax.ShapeDtypeStruct((tok, width // 2), BF16),
            jax.ShapeDtypeStruct((2, width // 2, length), BF16),
            jax.ShapeDtypeStruct((3, width, width // 2), BF16),
            jax.ShapeDtypeStruct((1, width), F32),
            jax.ShapeDtypeStruct((pairs, 2, wide), F32),
        ],
        compiler_params=pltpu.CompilerParams(vmem_limit_bytes=56 * MIB),
        cost_estimate=pl.CostEstimate(
            flops=4 * length * width * width + 8 * tok * length * width,
            bytes_accessed=8 * length * width + 2 * pairs * tok * length,
            transcendentals=0,
        ),
        name="attend_back",
    )(half, probs, grad_heads, heads, query, key, value, act_all, act, *turned, ready)


def spread_kernel(half_ref, wka_ref, wva_ref, a_ref, wkb_ref, wvb_ref, b_ref, out_ref):
    tok = out_ref.shape[2]
    found = mm(jnp.concatenate([wka_ref[...], wva_ref[...]], 1), jnp.concatenate([a_ref[0], a_ref[1]], 0))
    found += mm(jnp.concatenate([wkb_ref[...], wvb_ref[...]], 1), jnp.concatenate([b_ref[0], b_ref[1]], 0))
    found = found.astype(BF16)
    for i in range(out_ref.shape[0]):
        out_ref[i] = found[:, i * tok : (i + 1) * tok]


def spread(half, w_key, w_value, terms_a, terms_b, tok):
    width = w_key.shape[0]
    length = terms_a.shape[2]
    cols = width // 2
    weight_a = pl.BlockSpec((width, cols), lambda c, h: (0, h[0]))
    weight_b = pl.BlockSpec((width, cols), lambda c, h: (0, 1 - h[0]))
    terms = pl.BlockSpec((2, cols, 2 * tok), lambda c, h: (0, 0, c))
    return pl.pallas_call(
        spread_kernel,
        grid_spec=pltpu.PrefetchScalarGridSpec(
            num_scalar_prefetch=1,
            grid=(length // (2 * tok),),
            in_specs=[weight_a, weight_a, terms, weight_b, weight_b, terms],
            out_specs=pl.BlockSpec((2, width, tok), lambda c, h: (c, 0, 0)),
        ),
        out_shape=jax.ShapeDtypeStruct((length // tok, width, tok), BF16),
        compiler_params=pltpu.CompilerParams(vmem_limit_bytes=56 * MIB),
        cost_estimate=pl.CostEstimate(
            flops=4 * length * width * width, bytes_accessed=6 * length * width, transcendentals=0
        ),
        name="spread",
    )(half, w_key, w_value, terms_a, w_key, w_value, terms_b)


def merge_kernel(mine_ref, other_ref, mine_out_ref, other_out_ref, small_ref, out_ref):
    count = out_ref.shape[0]
    rows = mine_ref.shape[1] // count
    for c in range(count):
        here = slice(c * rows, (c + 1) * rows)
        for i in range(3):
            found = mine_ref[i, here, :].astype(F32) + other_ref[i, here, :].astype(F32)
            out_ref[c, i * rows : (i + 1) * rows, :] = found.astype(BF16)
        found = mine_out_ref[here, :].astype(F32) + other_out_ref[here, :].astype(F32)
        out_ref[c, 3 * rows : 4 * rows, :] = found.astype(BF16)
        out_ref[c, 4 * rows :, :] = small_ref[c]


def merge_halves(mine, other, mine_out, other_out, small):
    count, extra, cols = small.shape
    width = mine.shape[1]
    rows = width // count
    steps = 4
    each = count // steps
    triple = pl.BlockSpec((3, each * rows, cols), lambda c: (0, c, 0))
    single = pl.BlockSpec((each * rows, cols), lambda c: (c, 0))
    return pl.pallas_call(
        merge_kernel,
        grid=(steps,),
        in_specs=[triple, triple, single, single, pl.BlockSpec((each, extra, cols), lambda c: (c, 0, 0))],
        out_specs=pl.BlockSpec((each, 4 * rows + extra, cols), lambda c: (c, 0, 0)),
        out_shape=jax.ShapeDtypeStruct((count, 4 * rows + extra, cols), BF16),
        compiler_params=pltpu.CompilerParams(vmem_limit_bytes=56 * MIB),
        name="merge_halves",
    )(mine, other, mine_out, other_out, small)


def unpack_kernel(core_ref, mine_ref, other_ref, *out_refs):
    count = mine_ref.shape[0]
    rows, width = out_refs[0].shape
    rows = rows // count
    cols = width // 2
    low = core_ref[0] == 0
    for c in range(count):
        for i, out_ref in enumerate(out_refs):
            mine = mine_ref[c, i * rows : (i + 1) * rows, :].astype(F32)
            other = other_ref[c, i * rows : (i + 1) * rows, :].astype(F32)
            out_ref[c * rows : (c + 1) * rows, :cols] = jnp.where(low, mine, other)
            out_ref[c * rows : (c + 1) * rows, cols:] = jnp.where(low, other, mine)


def unpack_halves(core, mine, other):
    count, total, cols = mine.shape
    width = 2 * cols
    rows = width // count
    steps = 4
    each = count // steps
    block = pl.BlockSpec((each, total, cols), lambda c, core: (c, 0, 0))
    return pl.pallas_call(
        unpack_kernel,
        grid_spec=pltpu.PrefetchScalarGridSpec(
            num_scalar_prefetch=1,
            grid=(steps,),
            in_specs=[block, block],
            out_specs=[pl.BlockSpec((each * rows, width), lambda c, core: (c, 0))] * 4,
        ),
        out_shape=[jax.ShapeDtypeStruct((width, width), F32)] * 4,
        compiler_params=pltpu.CompilerParams(vmem_limit_bytes=56 * MIB),
        name="unpack_halves",
    )(core, mine, other)


def expert_kernel(rows_ref, win_ref, wout_ref, out_ref, total_ref):
    width = win_ref.shape[0]
    step = pl.program_id(0)
    sent = rows_ref[:, :width]
    grad = rows_ref[:, width:]
    hidden, slope = gelu_parts(mm(sent, win_ref[...]))
    grad_pre = (mm(grad, wout_ref[...], NT) * slope).astype(BF16)
    forward = mm(hidden.astype(BF16), wout_ref[...])
    backward = mm(grad_pre, win_ref[...], NT)

    @pl.when(step == 0)
    def _():
        total_ref[:, :width] = forward
        total_ref[:, width:] = backward

    @pl.when(step > 0)
    def _():
        total_ref[:, :width] += forward
        total_ref[:, width:] += backward

    @pl.when(step == pl.num_programs(0) - 1)
    def _():
        out_ref[...] = total_ref[...].astype(BF16)


def expert_both(rows, w_in, w_out):
    count, double = rows.shape
    width, units = w_in.shape
    chunk = 768 if units % 768 == 0 else units
    return pl.pallas_call(
        expert_kernel,
        grid=(units // chunk,),
        in_specs=[
            pl.BlockSpec((count, double), lambda c: (0, 0)),
            pl.BlockSpec((width, chunk), lambda c: (0, c)),
            pl.BlockSpec((chunk, width), lambda c: (c, 0)),
        ],
        out_specs=pl.BlockSpec((count, double), lambda c: (0, 0)),
        out_shape=jax.ShapeDtypeStruct((count, double), BF16),
        scratch_shapes=[pltpu.VMEM((count, double), F32)],
        compiler_params=pltpu.CompilerParams(vmem_limit_bytes=56 * MIB),
        cost_estimate=pl.CostEstimate(
            flops=8 * count * width * units, bytes_accessed=4 * width * units, transcendentals=count * units
        ),
        name="expert_both",
    )(rows, w_in, w_out)


def expert_grad_kernel(place_ref, *refs):
    row_refs, (wint_ref, wout_ref, out_ref) = refs[:-3], refs[-3:]
    width = wint_ref.shape[1]
    rows = jnp.concatenate([ref[...] for ref in row_refs], 0)
    sent = rows[:, :width]
    grad = rows[:, width:]
    hidden, slope = gelu_parts(mm(wint_ref[...], sent, NT))
    grad_pre = (mm(wout_ref[...], grad, NT) * slope).astype(BF16)
    found = (mm(grad_pre, sent).astype(BF16), mm(hidden.astype(BF16), grad).astype(BF16))
    share = out_ref.shape[3]
    for d in range(2):
        to = lax.rem(d + place_ref[1], 2)
        for i in range(2):
            out_ref[0, to, i] = found[i][d * share : (d + 1) * share]


def expert_grads(place, parts, w_in_t, w_out, side):
    units, width = w_out.shape
    count = sum(part.shape[0] for part in parts)
    chunk = units // side
    weight = pl.BlockSpec((chunk, width), lambda c, place: (c, 0))
    return pl.pallas_call(
        expert_grad_kernel,
        grid_spec=pltpu.PrefetchScalarGridSpec(
            num_scalar_prefetch=1,
            grid=(side,),
            in_specs=[pl.BlockSpec(part.shape, lambda c, place: (0, 0)) for part in parts] + [weight, weight],
            out_specs=pl.BlockSpec(
                (1, 2, 2, chunk // 2, width),
                lambda c, place: (lax.rem(c + side - place[0], side), 0, 0, 0, 0),
            ),
        ),
        out_shape=jax.ShapeDtypeStruct((side, 2, 2, chunk // 2, width), BF16),
        compiler_params=pltpu.CompilerParams(vmem_limit_bytes=56 * MIB),
        cost_estimate=pl.CostEstimate(
            flops=8 * count * width * units, bytes_accessed=8 * width * units, transcendentals=count * units
        ),
        name="expert_grads",
    )(place, *parts, w_in_t, w_out)


def per_device(
    ctx_count,
    dp_count,
    inputs,
    cotangent,
    norm1_gain,
    w_query,
    w_key,
    w_value,
    w_output,
    bias_table,
    buckets,
    norm2_gain,
    w_router,
    routes,
    w_in,
    w_out,
):
    tok_count, width = inputs.shape[1:]
    length = (buckets.shape[0] + 1) // 2
    bucket_count, head_count = bias_table.shape
    expert_count = w_router.shape[1]
    capacity = (tok_count * 5 + 4 * expert_count - 1) // (4 * expert_count)
    side = math.isqrt(ctx_count)
    units = w_in.shape[2]
    context = lax.axis_index("context")
    ctx_y, ctx_x = context // side, context % side
    dp = lax.axis_index("dp")

    def ring(values, along_y, step):
        pairs = []
        for c in range(ctx_count):
            y, x = divmod(c, side)
            to = ((y + step) % side) * side + x if along_y else y * side + (x + step) % side
            pairs.append((c, to))
        return lax.ppermute(values, "context", pairs)

    inputs_f = inputs[0].astype(F32)
    gain1 = norm1_gain.astype(F32)
    scale1 = rms_stats(inputs_f)
    act = (inputs_f * scale1 * gain1).astype(BF16)
    act_all = lax.all_gather(act, "context", axis=0, tiled=True)

    padded = jnp.pad(buckets, (0, 1))
    start = length - tok_count - context * tok_count
    near = lax.dynamic_slice_in_dim(padded, start, length + tok_count)
    onehot = (jnp.arange(bucket_count, dtype=jnp.int32)[:, None] == near[None, :]).astype(BF16)
    window = lax.dot_general(bias_table, onehot, (((0,), (0,)), ((), ())), preferred_element_type=F32)
    window = window.reshape(head_count // 2, 2, length + tok_count)

    route = routes[0, :, 0]
    chosen = (route[:, None] == jnp.arange(expert_count, dtype=jnp.int32)[None, :]).astype(jnp.int32)
    chosen_f = chosen.astype(F32)
    slot_of = jnp.sum((jnp.cumsum(chosen, axis=0) - 1) * chosen, axis=-1)
    target = route * capacity + slot_of
    slots = jnp.arange(expert_count * capacity, dtype=jnp.int32)
    dispatch = (slots[:, None] == target[None, :]).astype(BF16)
    collect = (target[:, None] == slots[None, :]).astype(BF16)
    quarter = units // side
    w_in_slice = lax.dynamic_slice_in_dim(w_in[0], ctx_y * quarter, quarter, 1).T
    w_out_slice = lax.dynamic_slice_in_dim(w_out[0], ctx_y * quarter, quarter, 0)

    turned = (w_query.T, w_key.T, w_value.T)
    ready = (w_in_slice, w_out_slice) + turned
    query, key, value, heads_f, inverse, probs = attend(
        act_all, act, w_query, w_key, w_value, window, ready
    )
    heads_out = heads_f.astype(BF16)
    resid = inputs_f + mm(heads_out, w_output)
    gain2 = norm2_gain.astype(F32)
    scale2 = rms_stats(resid)
    normed2 = resid * scale2 * gain2
    router = w_router.astype(F32)
    logits = jnp.dot(normed2, router, precision=HIGHEST)
    router_exp = jnp.exp(logits - jnp.max(logits, axis=-1, keepdims=True))
    router_probs = router_exp / jnp.sum(router_exp, axis=-1, keepdims=True)
    gate = jnp.sum(router_probs * chosen_f, axis=-1)
    grad_out = cotangent[0].astype(F32)
    grad_picked = gate[:, None] * grad_out
    going = jnp.concatenate([normed2.astype(BF16), grad_picked.astype(BF16)], 1)
    going = mm(dispatch, going).astype(BF16).reshape(expert_count, capacity, 2 * width)
    arrived = lax.all_to_all(going, "expert", split_axis=0, concat_axis=0, tiled=True)
    arrived = arrived.reshape(expert_count * capacity, 2 * width)
    results = expert_both(arrived, w_in[0], w_out[0])
    results = results.reshape(expert_count, capacity, 2 * width)
    returned = lax.all_to_all(results, "expert", split_axis=0, concat_axis=0, tiled=True)
    returned = mm(collect, returned.reshape(expert_count * capacity, 2 * width))
    picked, grad_sent = returned[:, :width], returned[:, width:]
    mixed = resid + gate[:, None] * picked

    parts = [arrived] + [ring(arrived, True, step) for step in range(1, side)]
    shares = expert_grads(jnp.stack([ctx_x, dp]).astype(jnp.int32), parts, w_in_slice, w_out_slice, side)
    expert_sum = shares[0, 0].astype(F32)
    for step in range(side):
        for flip in range(2):
            if step == 0 and flip == 0:
                continue
            route_pairs = []
            for c in range(ctx_count):
                to = c // side * side + (c % side + step) % side
                for d in range(2):
                    route_pairs.append((c * 2 + d, to * 2 + (d ^ flip)))
            moved = lax.ppermute(shares[step, flip], ("context", "dp"), route_pairs)
            expert_sum = expert_sum + moved.astype(F32)
    grad_w_in_out = expert_sum[0].T[None]
    grad_w_out_out = expert_sum[1][None]

    grad_gate = jnp.sum(grad_out * picked, axis=-1)
    grad_logits = (grad_gate * gate)[:, None] * (chosen_f - router_probs)
    grad_router = lax.dot_general(grad_logits, normed2, (((0,), (0,)), ((), ())), precision=HIGHEST)
    grad_normed2 = grad_sent + jnp.dot(grad_logits, router.T, precision=HIGHEST)
    grad_gain2 = jnp.sum(grad_normed2 * resid * scale2, axis=0)
    grad_resid = rms_back(grad_normed2, resid, scale2, gain2) + grad_out
    grad_attn = grad_resid.astype(BF16)
    grad_heads = mm(grad_attn, w_output, NT).astype(BF16)
    scaled = (grad_heads.astype(F32) * inverse).astype(BF16)

    expert = lax.axis_index("expert")
    core = (expert % 2)[None]
    swap = [(e, e ^ 1) for e in range(expert_count)]
    cols = width // 2
    both_out = []
    for half in (1 - core[0], core[0]):
        attn_half = lax.dynamic_slice_in_dim(grad_attn, half * cols, cols, 1)
        both_out.append(jnp.dot(heads_out.T, attn_half, preferred_element_type=F32).astype(BF16))
    other_out = lax.ppermute(both_out[0], "expert", swap)
    back = functools.partial(
        attend_back, probs=probs, grad_heads=scaled, heads=heads_f, query=query, key=key, value=value,
        act_all=act_all, act=act, turned=turned,
    )
    dq_a, terms_a, grads_a, gain_a, diag_a = back(1 - core, ready=arrived)
    other = lax.ppermute(grads_a, "expert", swap)
    dq_b, terms_b, grads_b, gain_b, diag_b = back(core, ready=shares)
    part = spread(core, w_key, w_value, terms_b, terms_a, tok_count)
    low = core[0] == 0
    in_order = lambda a, b, axis: jnp.concatenate([jnp.where(low, b, a), jnp.where(low, a, b)], axis)
    diagonals = in_order(diag_a, diag_b, 0)
    diagonals = diagonals.reshape(head_count, length + tok_count)
    grad_table = lax.dot_general(
        diagonals, onehot.astype(F32), (((1,), (1,)), ((), ())), precision=HIGHEST
    )
    small = jnp.concatenate(
        [(gain_a + gain_b)[0] / gain1, grad_gain2, grad_router.reshape(-1), grad_table.reshape(-1)]
    )
    small = jnp.pad(small, (0, ctx_count * 16 * cols - small.size)).astype(BF16)
    merged = merge_halves(grads_b, other, both_out[1], other_out, small.reshape(ctx_count, 16, cols))
    merged = lax.all_to_all(merged, "context", split_axis=0, concat_axis=0, tiled=True)
    merged = jnp.sum(merged.astype(F32), axis=0).astype(BF16)
    part, merged = lax.optimization_barrier((part, merged))
    total = merged.astype(F32)
    depth = expert_count // 2 * dp_count
    for step in range(1, depth):
        pairs = []
        for e in range(expert_count):
            for d in range(dp_count):
                z = (e // 2 * dp_count + d + step) % depth
                to = (z // dp_count * 2 + e % 2) * dp_count + z % dp_count
                pairs.append((e * dp_count + d, to))
        total = total + lax.ppermute(merged, ("expert", "dp"), pairs).astype(F32)
    whole = lax.all_gather(total.astype(BF16), "context", axis=0)
    other = lax.ppermute(whole, "expert", swap)
    grad_w_query, grad_w_key, grad_w_value, grad_w_output = unpack_halves(core, whole, other)
    rows = 4 * width // ctx_count
    small = (whole[:, rows:].astype(F32) + other[:, rows:].astype(F32)).reshape(-1)
    edges = [width, 2 * width, (2 + expert_count) * width, (2 + expert_count) * width + bucket_count * head_count]
    grad_gain1, grad_gain2, grad_router, grad_table = jnp.split(small[: edges[3]], edges[:3])
    grad_router = grad_router.reshape(expert_count, width).T
    grad_table = grad_table.reshape(head_count, bucket_count).T
    grad_query = in_order(dq_a, dq_b, 1)

    part = lax.all_to_all(part, "context", split_axis=0, concat_axis=0, tiled=True)
    grad_act = mm(grad_query, w_query, NT) + jnp.sum(part.astype(F32), axis=0).T
    grad_inputs = rms_back(grad_act, inputs_f, scale1, gain1) + grad_resid
    return (
        mixed[None].astype(BF16),
        grad_inputs[None].astype(BF16),
        grad_gain1,
        grad_w_query,
        grad_w_key,
        grad_w_value,
        grad_w_output,
        grad_table,
        grad_gain2,
        grad_router,
        grad_w_in_out,
        grad_w_out_out,
    )


def solution(mesh):
    tokens = P(("expert", "dp"), "context", None)
    return jax.shard_map(
        functools.partial(per_device, mesh.shape["context"], mesh.shape["dp"]),
        mesh=mesh,
        in_specs=(
            tokens, tokens, P(), P(), P(), P(), P(), P(), P(), P(), P(), tokens,
            P("expert", None, None), P("expert", None, None),
        ),
        out_specs=(
            tokens, tokens, P(), P(), P(), P(), P(), P(), P(), P(),
            P("expert", None, ("context", "dp")), P("expert", ("context", "dp"), None),
        ),
        check_vma=False,
    )
```

```python
import functools
import math

import jax
import jax.numpy as jnp
from jax import lax
from jax.experimental import pallas as pl
from jax.experimental.pallas import tpu as pltpu
from jax.sharding import PartitionSpec as P

EPS = 1e-06
F32 = jnp.float32
BF16 = jnp.bfloat16
NN = (((1,), (0,)), ((), ()))
NT = (((1,), (1,)), ((), ()))
HIGHEST = lax.Precision.HIGHEST
MIB = 1 << 20


def mm(left, right, dims=NN):
    return lax.dot_general(left, right, dims, preferred_element_type=F32)


def rms_stats(values):
    return lax.rsqrt(jnp.mean(values * values, axis=-1, keepdims=True) + EPS)


def rms_back(grad, values, scale, gain):
    weighted = grad * gain
    inner = jnp.mean(weighted * values, axis=-1, keepdims=True)
    return scale * weighted - values * (scale * scale * scale * inner)


def gelu_parts(u):
    c = math.sqrt(2.0 / math.pi)
    sq = u * u
    t = jnp.tanh(c * u * (1.0 + 0.044715 * sq))
    half = 0.5 * (1.0 + t)
    slope = half + (0.5 * c) * u * (1.0 - t * t) * (1.0 + (3 * 0.044715) * sq)
    return u * half, slope


def first_half(shape, size):
    return lax.broadcasted_iota(jnp.int32, shape, 1) < size


def split_pair(pair, size):
    first = first_half(pair.shape, size)
    zero = jnp.zeros_like(pair)
    return jnp.concatenate([jnp.where(first, pair, zero), jnp.where(first, zero, pair)], 0)


def join_pair(stacked, size):
    rows = stacked.shape[0] // 2
    return jnp.where(first_half((rows, 2 * size), size), stacked[:rows], stacked[rows:])


def attend_kernel(act_ref, own_ref, wq_ref, wk_ref, wv_ref, win_ref, *refs):
    q_ref, k_ref, v_ref, o_ref, inv_ref, p_ref, s_ref, m_ref, ext_ref = refs[-9:]
    tok = own_ref.shape[0]
    length = act_ref.shape[0]
    wide = win_ref.shape[2]
    lanes = wq_ref.shape[1]
    size = lanes // 2
    query = mm(own_ref[...], wq_ref[...]).astype(BF16)
    query = query.astype(F32) * (1.0 / math.sqrt(size))
    q_ref[...] = query.astype(BF16)
    both = mm(act_ref[...], jnp.concatenate([wk_ref[...], wv_ref[...]], 1)).astype(BF16)
    k_ref[...] = both[:, :lanes]
    v_ref[...] = both[:, lanes:]
    ext_ref[:, :lanes] = both[:, lanes:]
    ext_ref[:, lanes:] = jnp.ones((length, lanes), BF16)
    s_ref[...] = mm(split_pair(query, size).astype(BF16), k_ref[...], NT)
    sub = lax.broadcasted_iota(jnp.int32, (16, wide), 0)

    def first_band(head):
        band = jnp.broadcast_to(win_ref[0, head : head + 1, :], (16, wide))
        band = pltpu.roll(band, wide - (tok - 1), 1)
        for bit in (1, 2, 4, 8):
            band = jnp.where((sub & bit) != 0, pltpu.roll(band, bit, 1), band)
        return band

    def rows_of(head, r):
        return pl.ds(pl.multiple_of(head * tok + r * 16, 16), 16)

    def add_bias(r, bands):
        for head in range(2):
            rows = rows_of(head, r)
            s = s_ref[rows, :] + bands[head][:, :length]
            s_ref[rows, :] = s
            tops = [s[:, c : c + lanes] for c in range(0, length, lanes)]
            while len(tops) > 1:
                tops = [jnp.maximum(a, b) for a, b in zip(tops[::2], tops[1::2])]
            m_ref[rows, :] = tops[0]
        return tuple(pltpu.roll(band, 16, 1) for band in bands)

    def exponents(r, carry):
        for part in range(4):
            rows = rows_of(0, 4 * r + part)
            top = jnp.concatenate([m_ref[rows, :]] * (length // lanes), 1)
            p_ref[0, rows, :] = jnp.exp(s_ref[rows, :] - top).astype(BF16)
        return carry

    lax.fori_loop(0, tok // 16, add_bias, (first_band(0), first_band(1)))
    m_ref[...] = jnp.broadcast_to(jnp.max(m_ref[...], axis=1, keepdims=True), m_ref.shape)
    lax.fori_loop(0, tok // 32, exponents, 0)
    summed = mm(p_ref[0], ext_ref[...])
    inverse = 1.0 / join_pair(summed[:, lanes:], size)
    inv_ref[...] = inverse
    o_ref[...] = join_pair(summed[:, :lanes], size) * inverse


def attend(act_all, act, w_query, w_key, w_value, window, ready):
    length, width = act_all.shape
    tok = act.shape[0]
    pairs, _, wide = window.shape
    lanes = width // pairs
    column = lambda rows: pl.BlockSpec((rows, lanes), lambda p: (0, p))
    whole = lambda rows: pl.BlockSpec((rows, width), lambda p: (0, 0))
    return pl.pallas_call(
        attend_kernel,
        grid=(pairs,),
        in_specs=[
            whole(length), whole(tok), column(width), column(width), column(width),
            pl.BlockSpec((1, 2, wide), lambda p: (p, 0, 0)),
        ] + [pl.BlockSpec(memory_space=pl.ANY)] * len(ready),
        out_specs=[
            column(tok), column(length), column(length), column(tok), column(tok),
            pl.BlockSpec((1, 2 * tok, length), lambda p: (p, 0, 0)),
        ],
        out_shape=[
            jax.ShapeDtypeStruct((tok, width), BF16),
            jax.ShapeDtypeStruct((length, width), BF16),
            jax.ShapeDtypeStruct((length, width), BF16),
            jax.ShapeDtypeStruct((tok, width), F32),
            jax.ShapeDtypeStruct((tok, width), F32),
            jax.ShapeDtypeStruct((pairs, 2 * tok, length), BF16),
        ],
        scratch_shapes=[
            pltpu.VMEM((2 * tok, length), F32),
            pltpu.VMEM((2 * tok, lanes), F32),
            pltpu.VMEM((length, 2 * lanes), BF16),
        ],
        compiler_params=pltpu.CompilerParams(vmem_limit_bytes=56 * MIB),
        cost_estimate=pl.CostEstimate(
            flops=4 * length * width * width + 8 * tok * length * width,
            bytes_accessed=12 * length * width + 4 * pairs * tok * length,
            transcendentals=2 * pairs * tok * length,
        ),
        name="attend",
    )(act_all, act, w_query, w_key, w_value, window, *ready)


def attend_back_kernel(half_ref, p_ref, do_ref, o_ref, q_ref, k_ref, v_ref, act_ref, own_ref,
                       wqt_ref, wkt_ref, wvt_ref, ready_ref,
                       dq_ref, dkv_ref, grad_ref, gain_ref, diag_ref,
                       dp_ref, ds_ref, delta_ref):
    tok = do_ref.shape[0]
    length = act_ref.shape[0]
    lanes = q_ref.shape[1]
    wide = diag_ref.shape[2]
    size = lanes // 2
    pair = pl.program_id(0)
    grad = do_ref[...].astype(F32)
    grads = split_pair(grad, size)
    delta = jnp.sum(split_pair(grad * o_ref[...], size), axis=1, keepdims=True)
    delta_ref[...] = jnp.broadcast_to(delta, delta_ref.shape)
    dp_ref[...] = mm(grads.astype(BF16), v_ref[...], NT)

    def step(r, totals):
        after = []
        for head in range(2):
            rows = pl.ds(pl.multiple_of(head * tok + r * 16, 16), 16)
            less = jnp.concatenate([delta_ref[rows, :]] * (length // lanes), 1)
            d = p_ref[0, rows, :].astype(F32) * (dp_ref[rows, :] - less)
            ds_ref[rows, :] = d.astype(BF16)
            d = jnp.concatenate([d, jnp.zeros((16, wide - length), F32)], 1)
            after.append(pltpu.roll(totals[head], 16, 1) + d)
        return tuple(after)

    empty = jnp.zeros((16, wide), F32)
    totals = lax.fori_loop(0, tok // 16, step, (empty, empty))
    sub = lax.broadcasted_iota(jnp.int32, (16, wide), 0)
    for head in range(2):
        total = totals[head]
        for bit in (1, 2, 4, 8):
            total = jnp.where((sub & bit) == 0, pltpu.roll(total, bit, 1), total)
        diag_ref[0, head : head + 1, :] = jnp.sum(total, axis=0, keepdims=True)
    dq = join_pair(mm(ds_ref[...], k_ref[...]), size) * (1.0 / math.sqrt(size))
    dq_ref[...] = dq.astype(BF16)
    queries = split_pair(q_ref[...].astype(F32), size)
    dk = mm(queries.T.astype(BF16), ds_ref[...]).astype(BF16)
    dv = mm(grads.T.astype(BF16), p_ref[0]).astype(BF16)
    dkv_ref[0] = dk
    dkv_ref[1] = dv
    weights = mm(jnp.concatenate([dk, dv], 0), act_ref[...])
    parts = (mm(dq.T.astype(BF16), own_ref[...]), weights[:lanes], weights[lanes:])
    gain = jnp.zeros((1, act_ref.shape[1]), F32)
    for i, (found, turned) in enumerate(zip(parts, (wqt_ref, wkt_ref, wvt_ref))):
        grad_ref[i] = found.T.astype(BF16)
        gain = gain + jnp.sum(found * turned[...].astype(F32), axis=0, keepdims=True)

    @pl.when(pair == 0)
    def _():
        gain_ref[...] = gain

    @pl.when(pair > 0)
    def _():
        gain_ref[...] += gain


def attend_back(half, probs, grad_heads, heads, query, key, value, act_all, act, turned, ready):
    length, width = act_all.shape
    tok = query.shape[0]
    pairs = probs.shape[0] // 2
    wide = length + tok
    lanes = width // (2 * pairs)
    column = lambda rows: pl.BlockSpec((rows, lanes), lambda p, h: (0, p + h[0] * pairs))
    whole = lambda rows, cols: pl.BlockSpec((rows, cols), lambda p, h: (0, 0))
    row = pl.BlockSpec((lanes, width), lambda p, h: (p + h[0] * pairs, 0))
    return pl.pallas_call(
        attend_back_kernel,
        grid_spec=pltpu.PrefetchScalarGridSpec(
            num_scalar_prefetch=1,
            grid=(pairs,),
            in_specs=[
                pl.BlockSpec((1, 2 * tok, length), lambda p, h: (p + h[0] * pairs, 0, 0)),
                column(tok), column(tok), column(tok), column(length), column(length),
                whole(length, width), whole(tok, width),
                row, row, row, pl.BlockSpec(memory_space=pl.ANY),
            ],
            out_specs=[
                pl.BlockSpec((tok, lanes), lambda p, h: (0, p)),
                pl.BlockSpec((2, lanes, length), lambda p, h: (0, p, 0)),
                pl.BlockSpec((3, width, lanes), lambda p, h: (0, 0, p)),
                pl.BlockSpec((1, width), lambda p, h: (0, 0)),
                pl.BlockSpec((1, 2, wide), lambda p, h: (p, 0, 0)),
            ],
            scratch_shapes=[
                pltpu.VMEM((2 * tok, length), F32),
                pltpu.VMEM((2 * tok, length), BF16),
                pltpu.VMEM((2 * tok, lanes), F32),
            ],
        ),
        out_shape=[
            jax.ShapeDtypeStruct((tok, width // 2), BF16),
            jax.ShapeDtypeStruct((2, width // 2, length), BF16),
            jax.ShapeDtypeStruct((3, width, width // 2), BF16),
            jax.ShapeDtypeStruct((1, width), F32),
            jax.ShapeDtypeStruct((pairs, 2, wide), F32),
        ],
        compiler_params=pltpu.CompilerParams(vmem_limit_bytes=56 * MIB),
        cost_estimate=pl.CostEstimate(
            flops=4 * length * width * width + 8 * tok * length * width,
            bytes_accessed=8 * length * width + 2 * pairs * tok * length,
            transcendentals=0,
        ),
        name="attend_back",
    )(half, probs, grad_heads, heads, query, key, value, act_all, act, *turned, ready)


def spread_kernel(half_ref, wka_ref, wva_ref, a_ref, wkb_ref, wvb_ref, b_ref, *refs):
    out_ref = refs[-1]
    tok = out_ref.shape[2]
    found = mm(jnp.concatenate([wka_ref[...], wva_ref[...]], 1), jnp.concatenate([a_ref[0], a_ref[1]], 0))
    found += mm(jnp.concatenate([wkb_ref[...], wvb_ref[...]], 1), jnp.concatenate([b_ref[0], b_ref[1]], 0))
    found = found.astype(BF16)
    for i in range(out_ref.shape[0]):
        out_ref[i] = found[:, i * tok : (i + 1) * tok]


def spread(half, w_key, w_value, terms_a, terms_b, tok, ready):
    width = w_key.shape[0]
    length = terms_a.shape[2]
    cols = width // 2
    weight_a = pl.BlockSpec((width, cols), lambda c, h: (0, h[0]))
    weight_b = pl.BlockSpec((width, cols), lambda c, h: (0, 1 - h[0]))
    terms = pl.BlockSpec((2, cols, 2 * tok), lambda c, h: (0, 0, c))
    return pl.pallas_call(
        spread_kernel,
        grid_spec=pltpu.PrefetchScalarGridSpec(
            num_scalar_prefetch=1,
            grid=(length // (2 * tok),),
            in_specs=[weight_a, weight_a, terms, weight_b, weight_b, terms]
            + [pl.BlockSpec(memory_space=pl.ANY)] * len(ready),
            out_specs=pl.BlockSpec((2, width, tok), lambda c, h: (c, 0, 0)),
        ),
        out_shape=jax.ShapeDtypeStruct((length // tok, width, tok), BF16),
        compiler_params=pltpu.CompilerParams(vmem_limit_bytes=56 * MIB),
        cost_estimate=pl.CostEstimate(
            flops=4 * length * width * width, bytes_accessed=6 * length * width, transcendentals=0
        ),
        name="spread",
    )(half, w_key, w_value, terms_a, w_key, w_value, terms_b, *ready)


def merge_kernel(mine_ref, other_ref, mine_out_ref, other_out_ref, small_ref, out_ref):
    count = out_ref.shape[0]
    rows = mine_ref.shape[1] // count
    for c in range(count):
        here = slice(c * rows, (c + 1) * rows)
        for i in range(3):
            found = mine_ref[i, here, :].astype(F32) + other_ref[i, here, :].astype(F32)
            out_ref[c, i * rows : (i + 1) * rows, :] = found.astype(BF16)
        found = mine_out_ref[here, :].astype(F32) + other_out_ref[here, :].astype(F32)
        out_ref[c, 3 * rows : 4 * rows, :] = found.astype(BF16)
        out_ref[c, 4 * rows :, :] = small_ref[c]


def merge_halves(mine, other, mine_out, other_out, small):
    count, extra, cols = small.shape
    width = mine.shape[1]
    rows = width // count
    steps = 4
    each = count // steps
    triple = pl.BlockSpec((3, each * rows, cols), lambda c: (0, c, 0))
    single = pl.BlockSpec((each * rows, cols), lambda c: (c, 0))
    return pl.pallas_call(
        merge_kernel,
        grid=(steps,),
        in_specs=[triple, triple, single, single, pl.BlockSpec((each, extra, cols), lambda c: (c, 0, 0))],
        out_specs=pl.BlockSpec((each, 4 * rows + extra, cols), lambda c: (c, 0, 0)),
        out_shape=jax.ShapeDtypeStruct((count, 4 * rows + extra, cols), BF16),
        compiler_params=pltpu.CompilerParams(vmem_limit_bytes=56 * MIB),
        name="merge_halves",
    )(mine, other, mine_out, other_out, small)


def unpack_kernel(core_ref, mine_ref, other_ref, *out_refs):
    count = mine_ref.shape[0]
    rows, width = out_refs[0].shape
    rows = rows // count
    cols = width // 2
    low = core_ref[0] == 0
    for c in range(count):
        for i, out_ref in enumerate(out_refs):
            mine = mine_ref[c, i * rows : (i + 1) * rows, :].astype(F32)
            other = other_ref[c, i * rows : (i + 1) * rows, :].astype(F32)
            out_ref[c * rows : (c + 1) * rows, :cols] = jnp.where(low, mine, other)
            out_ref[c * rows : (c + 1) * rows, cols:] = jnp.where(low, other, mine)


def unpack_halves(core, mine, other):
    count, total, cols = mine.shape
    width = 2 * cols
    rows = width // count
    steps = 4
    each = count // steps
    block = pl.BlockSpec((each, total, cols), lambda c, core: (c, 0, 0))
    return pl.pallas_call(
        unpack_kernel,
        grid_spec=pltpu.PrefetchScalarGridSpec(
            num_scalar_prefetch=1,
            grid=(steps,),
            in_specs=[block, block],
            out_specs=[pl.BlockSpec((each * rows, width), lambda c, core: (c, 0))] * 4,
        ),
        out_shape=[jax.ShapeDtypeStruct((width, width), F32)] * 4,
        compiler_params=pltpu.CompilerParams(vmem_limit_bytes=56 * MIB),
        name="unpack_halves",
    )(core, mine, other)


def expert_kernel(rows_ref, win_ref, wout_ref, out_ref, total_ref):
    width = win_ref.shape[0]
    step = pl.program_id(0)
    sent = rows_ref[:, :width]
    grad = rows_ref[:, width:]
    hidden, slope = gelu_parts(mm(sent, win_ref[...]))
    grad_pre = (mm(grad, wout_ref[...], NT) * slope).astype(BF16)
    forward = mm(hidden.astype(BF16), wout_ref[...])
    backward = mm(grad_pre, win_ref[...], NT)

    @pl.when(step == 0)
    def _():
        total_ref[:, :width] = forward
        total_ref[:, width:] = backward

    @pl.when(step > 0)
    def _():
        total_ref[:, :width] += forward
        total_ref[:, width:] += backward

    @pl.when(step == pl.num_programs(0) - 1)
    def _():
        out_ref[...] = total_ref[...].astype(BF16)


def expert_both(rows, w_in, w_out):
    count, double = rows.shape
    width, units = w_in.shape
    chunk = 768 if units % 768 == 0 else units
    return pl.pallas_call(
        expert_kernel,
        grid=(units // chunk,),
        in_specs=[
            pl.BlockSpec((count, double), lambda c: (0, 0)),
            pl.BlockSpec((width, chunk), lambda c: (0, c)),
            pl.BlockSpec((chunk, width), lambda c: (c, 0)),
        ],
        out_specs=pl.BlockSpec((count, double), lambda c: (0, 0)),
        out_shape=jax.ShapeDtypeStruct((count, double), BF16),
        scratch_shapes=[pltpu.VMEM((count, double), F32)],
        compiler_params=pltpu.CompilerParams(vmem_limit_bytes=56 * MIB),
        cost_estimate=pl.CostEstimate(
            flops=8 * count * width * units, bytes_accessed=4 * width * units, transcendentals=count * units
        ),
        name="expert_both",
    )(rows, w_in, w_out)


def expert_grad_kernel(place_ref, *refs):
    row_refs, (wint_ref, wout_ref, out_ref, rows_ref) = refs[:-4], refs[-4:]
    width = wint_ref.shape[1]
    count = row_refs[0].shape[0]

    @pl.when(pl.program_id(0) == 0)
    def _():
        for i, ref in enumerate(row_refs):
            rows_ref[i * count : (i + 1) * count, :] = ref[...]

    sent = rows_ref[:, :width]
    grad = rows_ref[:, width:]
    hidden, slope = gelu_parts(mm(wint_ref[...], sent, NT))
    grad_pre = (mm(wout_ref[...], grad, NT) * slope).astype(BF16)
    found = (mm(grad_pre, sent).astype(BF16), mm(hidden.astype(BF16), grad).astype(BF16))
    share = out_ref.shape[3]
    for d in range(2):
        to = lax.rem(d + place_ref[1], 2)
        for i in range(2):
            out_ref[0, to, i] = found[i][d * share : (d + 1) * share]


def expert_grads(place, parts, w_in_t, w_out, side):
    units, width = w_out.shape
    count = sum(part.shape[0] for part in parts)
    chunk = units // side
    weight = pl.BlockSpec((chunk, width), lambda c, place: (c, 0))
    return pl.pallas_call(
        expert_grad_kernel,
        grid_spec=pltpu.PrefetchScalarGridSpec(
            num_scalar_prefetch=1,
            grid=(side,),
            in_specs=[pl.BlockSpec(part.shape, lambda c, place: (0, 0)) for part in parts] + [weight, weight],
            out_specs=pl.BlockSpec(
                (1, 2, 2, chunk // 2, width),
                lambda c, place: (lax.rem(c + side - place[0], side), 0, 0, 0, 0),
            ),
            scratch_shapes=[pltpu.VMEM((count, 2 * width), BF16)],
        ),
        out_shape=jax.ShapeDtypeStruct((side, 2, 2, chunk // 2, width), BF16),
        compiler_params=pltpu.CompilerParams(vmem_limit_bytes=56 * MIB),
        cost_estimate=pl.CostEstimate(
            flops=8 * count * width * units, bytes_accessed=8 * width * units, transcendentals=count * units
        ),
        name="expert_grads",
    )(place, *parts, w_in_t, w_out)


def per_device(
    ctx_count,
    dp_count,
    inputs,
    cotangent,
    norm1_gain,
    w_query,
    w_key,
    w_value,
    w_output,
    bias_table,
    buckets,
    norm2_gain,
    w_router,
    routes,
    w_in,
    w_out,
):
    tok_count, width = inputs.shape[1:]
    length = (buckets.shape[0] + 1) // 2
    bucket_count, head_count = bias_table.shape
    expert_count = w_router.shape[1]
    capacity = (tok_count * 5 + 4 * expert_count - 1) // (4 * expert_count)
    side = math.isqrt(ctx_count)
    units = w_in.shape[2]
    context = lax.axis_index("context")
    ctx_y, ctx_x = context // side, context % side
    dp = lax.axis_index("dp")

    def ring(values, along_y, step):
        pairs = []
        for c in range(ctx_count):
            y, x = divmod(c, side)
            to = ((y + step) % side) * side + x if along_y else y * side + (x + step) % side
            pairs.append((c, to))
        return lax.ppermute(values, "context", pairs)

    inputs_f = inputs[0].astype(F32)
    gain1 = norm1_gain.astype(F32)
    scale1 = rms_stats(inputs_f)
    act = (inputs_f * scale1 * gain1).astype(BF16)
    act_all = lax.all_gather(act, "context", axis=0, tiled=True)

    padded = jnp.pad(buckets, (0, 1))
    start = length - tok_count - context * tok_count
    near = lax.dynamic_slice_in_dim(padded, start, length + tok_count)
    onehot = (jnp.arange(bucket_count, dtype=jnp.int32)[:, None] == near[None, :]).astype(BF16)
    window = lax.dot_general(bias_table, onehot, (((0,), (0,)), ((), ())), preferred_element_type=F32)
    window = window.reshape(head_count // 2, 2, length + tok_count)

    route = routes[0, :, 0]
    chosen = (route[:, None] == jnp.arange(expert_count, dtype=jnp.int32)[None, :]).astype(jnp.int32)
    chosen_f = chosen.astype(F32)
    slot_of = jnp.sum((jnp.cumsum(chosen, axis=0) - 1) * chosen, axis=-1)
    target = route * capacity + slot_of
    slots = jnp.arange(expert_count * capacity, dtype=jnp.int32)
    dispatch = (slots[:, None] == target[None, :]).astype(BF16)
    collect = (target[:, None] == slots[None, :]).astype(BF16)
    quarter = units // side
    w_in_slice = lax.dynamic_slice_in_dim(w_in[0], ctx_y * quarter, quarter, 1).T
    w_out_slice = lax.dynamic_slice_in_dim(w_out[0], ctx_y * quarter, quarter, 0)

    turned = (w_query.T, w_key.T, w_value.T)
    ready = (w_in_slice, w_out_slice) + turned
    query, key, value, heads_f, inverse, probs = attend(
        act_all, act, w_query, w_key, w_value, window, ready
    )
    heads_out = heads_f.astype(BF16)
    resid = inputs_f + mm(heads_out, w_output)
    gain2 = norm2_gain.astype(F32)
    scale2 = rms_stats(resid)
    normed2 = resid * scale2 * gain2
    router = w_router.astype(F32)
    logits = jnp.dot(normed2, router, precision=HIGHEST)
    router_exp = jnp.exp(logits - jnp.max(logits, axis=-1, keepdims=True))
    router_probs = router_exp / jnp.sum(router_exp, axis=-1, keepdims=True)
    gate = jnp.sum(router_probs * chosen_f, axis=-1)
    grad_out = cotangent[0].astype(F32)
    grad_picked = gate[:, None] * grad_out
    going = jnp.concatenate([normed2.astype(BF16), grad_picked.astype(BF16)], 1)
    going = mm(dispatch, going).astype(BF16).reshape(expert_count, capacity, 2 * width)
    arrived = lax.all_to_all(going, "expert", split_axis=0, concat_axis=0, tiled=True)
    arrived = arrived.reshape(expert_count * capacity, 2 * width)
    results = expert_both(arrived, w_in[0], w_out[0])
    results = results.reshape(expert_count, capacity, 2 * width)
    returned = lax.all_to_all(results, "expert", split_axis=0, concat_axis=0, tiled=True)
    returned = mm(collect, returned.reshape(expert_count * capacity, 2 * width))
    picked, grad_sent = returned[:, :width], returned[:, width:]
    mixed = resid + gate[:, None] * picked

    parts = [arrived] + [ring(arrived, True, step) for step in range(1, side)]
    shares = expert_grads(jnp.stack([ctx_x, dp]).astype(jnp.int32), parts, w_in_slice, w_out_slice, side)
    expert_sum = shares[0, 0].astype(F32)
    for step in range(side):
        for flip in range(2):
            if step == 0 and flip == 0:
                continue
            route_pairs = []
            for c in range(ctx_count):
                to = c // side * side + (c % side + step) % side
                for d in range(2):
                    route_pairs.append((c * 2 + d, to * 2 + (d ^ flip)))
            moved = lax.ppermute(shares[step, flip], ("context", "dp"), route_pairs)
            expert_sum = expert_sum + moved.astype(F32)
    grad_w_in_out = expert_sum[0].T[None]
    grad_w_out_out = expert_sum[1][None]

    grad_gate = jnp.sum(grad_out * picked, axis=-1)
    grad_logits = (grad_gate * gate)[:, None] * (chosen_f - router_probs)
    grad_router = lax.dot_general(grad_logits, normed2, (((0,), (0,)), ((), ())), precision=HIGHEST)
    grad_normed2 = grad_sent + jnp.dot(grad_logits, router.T, precision=HIGHEST)
    grad_gain2 = jnp.sum(grad_normed2 * resid * scale2, axis=0)
    grad_resid = rms_back(grad_normed2, resid, scale2, gain2) + grad_out
    grad_attn = grad_resid.astype(BF16)
    grad_heads = mm(grad_attn, w_output, NT).astype(BF16)
    scaled = (grad_heads.astype(F32) * inverse).astype(BF16)

    expert = lax.axis_index("expert")
    core = (expert % 2)[None]
    swap = [(e, e ^ 1) for e in range(expert_count)]
    cols = width // 2
    both_out = []
    for half in (1 - core[0], core[0]):
        attn_half = lax.dynamic_slice_in_dim(grad_attn, half * cols, cols, 1)
        both_out.append(jnp.dot(heads_out.T, attn_half, preferred_element_type=F32).astype(BF16))
    other_out = lax.ppermute(both_out[0], "expert", swap)
    back = functools.partial(
        attend_back, probs=probs, grad_heads=scaled, heads=heads_f, query=query, key=key, value=value,
        act_all=act_all, act=act, turned=turned,
    )
    dq_a, terms_a, grads_a, gain_a, diag_a = back(1 - core, ready=arrived)
    other = lax.ppermute(grads_a, "expert", swap)
    dq_b, terms_b, grads_b, gain_b, diag_b = back(core, ready=shares)
    low = core[0] == 0
    in_order = lambda a, b, axis: jnp.concatenate([jnp.where(low, b, a), jnp.where(low, a, b)], axis)
    diagonals = in_order(diag_a, diag_b, 0)
    diagonals = diagonals.reshape(head_count, length + tok_count)
    grad_table = lax.dot_general(
        diagonals, onehot.astype(F32), (((1,), (1,)), ((), ())), precision=HIGHEST
    )
    small = jnp.concatenate(
        [(gain_a + gain_b)[0] / gain1, grad_gain2, grad_router.reshape(-1), grad_table.reshape(-1)]
    )
    small = jnp.pad(small, (0, ctx_count * 16 * cols - small.size)).astype(BF16)
    merged = merge_halves(grads_b, other, both_out[1], other_out, small.reshape(ctx_count, 16, cols))
    part = spread(core, w_key, w_value, terms_b, terms_a, tok_count, (expert_sum, merged))
    merged = lax.all_to_all(merged, "context", split_axis=0, concat_axis=0, tiled=True)
    merged = jnp.sum(merged.astype(F32), axis=0).astype(BF16)
    part, merged = lax.optimization_barrier((part, merged))
    total = merged.astype(F32)
    depth = expert_count // 2 * dp_count
    for step in range(1, depth):
        pairs = []
        for e in range(expert_count):
            for d in range(dp_count):
                z = (e // 2 * dp_count + d + step) % depth
                to = (z // dp_count * 2 + e % 2) * dp_count + z % dp_count
                pairs.append((e * dp_count + d, to))
        total = total + lax.ppermute(merged, ("expert", "dp"), pairs).astype(F32)
    whole = lax.all_gather(total.astype(BF16), "context", axis=0)
    other = lax.ppermute(whole, "expert", swap)
    grad_w_query, grad_w_key, grad_w_value, grad_w_output = unpack_halves(core, whole, other)
    rows = 4 * width // ctx_count
    small = (whole[:, rows:].astype(F32) + other[:, rows:].astype(F32)).reshape(-1)
    edges = [width, 2 * width, (2 + expert_count) * width, (2 + expert_count) * width + bucket_count * head_count]
    grad_gain1, grad_gain2, grad_router, grad_table = jnp.split(small[: edges[3]], edges[:3])
    grad_router = grad_router.reshape(expert_count, width).T
    grad_table = grad_table.reshape(head_count, bucket_count).T
    grad_query = in_order(dq_a, dq_b, 1)

    part = lax.all_to_all(part, "context", split_axis=0, concat_axis=0, tiled=True)
    grad_act = mm(grad_query, w_query, NT) + jnp.sum(part.astype(F32), axis=0).T
    grad_inputs = rms_back(grad_act, inputs_f, scale1, gain1) + grad_resid
    return (
        mixed[None].astype(BF16),
        grad_inputs[None].astype(BF16),
        grad_gain1,
        grad_w_query,
        grad_w_key,
        grad_w_value,
        grad_w_output,
        grad_table,
        grad_gain2,
        grad_router,
        grad_w_in_out,
        grad_w_out_out,
    )


def solution(mesh):
    tokens = P(("expert", "dp"), "context", None)
    return jax.shard_map(
        functools.partial(per_device, mesh.shape["context"], mesh.shape["dp"]),
        mesh=mesh,
        in_specs=(
            tokens, tokens, P(), P(), P(), P(), P(), P(), P(), P(), P(), tokens,
            P("expert", None, None), P("expert", None, None),
        ),
        out_specs=(
            tokens, tokens, P(), P(), P(), P(), P(), P(), P(), P(),
            P("expert", None, ("context", "dp")), P("expert", ("context", "dp"), None),
        ),
        check_vma=False,
    )
```

```python
import functools
import math

import jax
import jax.numpy as jnp
from jax import lax
from jax.experimental import pallas as pl
from jax.experimental.pallas import tpu as pltpu
from jax.sharding import PartitionSpec as P

EPS = 1e-06
F32 = jnp.float32
BF16 = jnp.bfloat16
NN = (((1,), (0,)), ((), ()))
NT = (((1,), (1,)), ((), ()))
HIGHEST = lax.Precision.HIGHEST
MIB = 1 << 20


def mm(left, right, dims=NN):
    return lax.dot_general(left, right, dims, preferred_element_type=F32)


def rms_stats(values):
    return lax.rsqrt(jnp.mean(values * values, axis=-1, keepdims=True) + EPS)


def rms_back(grad, values, scale, gain):
    weighted = grad * gain
    inner = jnp.mean(weighted * values, axis=-1, keepdims=True)
    return scale * weighted - values * (scale * scale * scale * inner)


def gelu_parts(u):
    c = math.sqrt(2.0 / math.pi)
    sq = u * u
    t = jnp.tanh(c * u * (1.0 + 0.044715 * sq))
    half = 0.5 * (1.0 + t)
    slope = half + (0.5 * c) * u * (1.0 - t * t) * (1.0 + (3 * 0.044715) * sq)
    return u * half, slope


def first_half(shape, size):
    return lax.broadcasted_iota(jnp.int32, shape, 1) < size


def split_pair(pair, size):
    first = first_half(pair.shape, size)
    zero = jnp.zeros_like(pair)
    return jnp.concatenate([jnp.where(first, pair, zero), jnp.where(first, zero, pair)], 0)


def join_pair(stacked, size):
    rows = stacked.shape[0] // 2
    return jnp.where(first_half((rows, 2 * size), size), stacked[:rows], stacked[rows:])


def attend_kernel(act_ref, own_ref, wq_ref, wk_ref, wv_ref, win_ref, *refs):
    q_ref, k_ref, v_ref, o_ref, inv_ref, p_ref, s_ref, m_ref, ext_ref = refs[-9:]
    tok = own_ref.shape[0]
    length = act_ref.shape[0]
    wide = win_ref.shape[2]
    lanes = wq_ref.shape[1]
    size = lanes // 2
    query = mm(own_ref[...], wq_ref[...]).astype(BF16)
    query = query.astype(F32) * (1.0 / math.sqrt(size))
    q_ref[...] = query.astype(BF16)
    both = mm(act_ref[...], jnp.concatenate([wk_ref[...], wv_ref[...]], 1)).astype(BF16)
    k_ref[...] = both[:, :lanes]
    v_ref[...] = both[:, lanes:]
    ext_ref[:, :lanes] = both[:, lanes:]
    ext_ref[:, lanes:] = jnp.ones((length, lanes), BF16)
    s_ref[...] = mm(split_pair(query, size).astype(BF16), k_ref[...], NT)
    sub = lax.broadcasted_iota(jnp.int32, (16, wide), 0)

    def first_band(head):
        band = jnp.broadcast_to(win_ref[0, head : head + 1, :], (16, wide))
        band = pltpu.roll(band, wide - (tok - 1), 1)
        for bit in (1, 2, 4, 8):
            band = jnp.where((sub & bit) != 0, pltpu.roll(band, bit, 1), band)
        return band

    def rows_of(head, r):
        return pl.ds(pl.multiple_of(head * tok + r * 16, 16), 16)

    def add_bias(r, bands):
        for head in range(2):
            rows = rows_of(head, r)
            s = s_ref[rows, :] + bands[head][:, :length]
            s_ref[rows, :] = s
            tops = [s[:, c : c + lanes] for c in range(0, length, lanes)]
            while len(tops) > 1:
                tops = [jnp.maximum(a, b) for a, b in zip(tops[::2], tops[1::2])]
            m_ref[rows, :] = tops[0]
        return tuple(pltpu.roll(band, 16, 1) for band in bands)

    def exponents(r, carry):
        for part in range(4):
            rows = rows_of(0, 4 * r + part)
            top = jnp.concatenate([m_ref[rows, :]] * (length // lanes), 1)
            p_ref[0, rows, :] = jnp.exp(s_ref[rows, :] - top).astype(BF16)
        return carry

    lax.fori_loop(0, tok // 16, add_bias, (first_band(0), first_band(1)))
    m_ref[...] = jnp.broadcast_to(jnp.max(m_ref[...], axis=1, keepdims=True), m_ref.shape)
    lax.fori_loop(0, tok // 32, exponents, 0)
    summed = mm(p_ref[0], ext_ref[...])
    inverse = 1.0 / join_pair(summed[:, lanes:], size)
    inv_ref[...] = inverse
    o_ref[...] = join_pair(summed[:, :lanes], size) * inverse


def attend(act_all, act, w_query, w_key, w_value, window, ready):
    length, width = act_all.shape
    tok = act.shape[0]
    pairs, _, wide = window.shape
    lanes = width // pairs
    column = lambda rows: pl.BlockSpec((rows, lanes), lambda p: (0, p))
    whole = lambda rows: pl.BlockSpec((rows, width), lambda p: (0, 0))
    return pl.pallas_call(
        attend_kernel,
        grid=(pairs,),
        in_specs=[
            whole(length), whole(tok), column(width), column(width), column(width),
            pl.BlockSpec((1, 2, wide), lambda p: (p, 0, 0)),
        ] + [pl.BlockSpec(memory_space=pl.ANY)] * len(ready),
        out_specs=[
            column(tok), column(length), column(length), column(tok), column(tok),
            pl.BlockSpec((1, 2 * tok, length), lambda p: (p, 0, 0)),
        ],
        out_shape=[
            jax.ShapeDtypeStruct((tok, width), BF16),
            jax.ShapeDtypeStruct((length, width), BF16),
            jax.ShapeDtypeStruct((length, width), BF16),
            jax.ShapeDtypeStruct((tok, width), F32),
            jax.ShapeDtypeStruct((tok, width), F32),
            jax.ShapeDtypeStruct((pairs, 2 * tok, length), BF16),
        ],
        scratch_shapes=[
            pltpu.VMEM((2 * tok, length), F32),
            pltpu.VMEM((2 * tok, lanes), F32),
            pltpu.VMEM((length, 2 * lanes), BF16),
        ],
        compiler_params=pltpu.CompilerParams(vmem_limit_bytes=56 * MIB),
        cost_estimate=pl.CostEstimate(
            flops=4 * length * width * width + 8 * tok * length * width,
            bytes_accessed=12 * length * width + 4 * pairs * tok * length,
            transcendentals=2 * pairs * tok * length,
        ),
        name="attend",
    )(act_all, act, w_query, w_key, w_value, window, *ready)


def attend_back_kernel(half_ref, p_ref, do_ref, o_ref, q_ref, k_ref, v_ref, act_ref, own_ref,
                       wqt_ref, wkt_ref, wvt_ref, ready_ref,
                       dq_ref, dkv_ref, grad_ref, gain_ref, diag_ref,
                       dp_ref, ds_ref, delta_ref):
    tok = do_ref.shape[0]
    length = act_ref.shape[0]
    lanes = q_ref.shape[1]
    wide = diag_ref.shape[2]
    size = lanes // 2
    pair = pl.program_id(0)
    grad = do_ref[...].astype(F32)
    grads = split_pair(grad, size)
    delta = jnp.sum(split_pair(grad * o_ref[...], size), axis=1, keepdims=True)
    delta_ref[...] = jnp.broadcast_to(delta, delta_ref.shape)
    dp_ref[...] = mm(grads.astype(BF16), v_ref[...], NT)

    def step(r, totals):
        after = []
        for head in range(2):
            rows = pl.ds(pl.multiple_of(head * tok + r * 16, 16), 16)
            less = jnp.concatenate([delta_ref[rows, :]] * (length // lanes), 1)
            d = p_ref[0, rows, :].astype(F32) * (dp_ref[rows, :] - less)
            ds_ref[rows, :] = d.astype(BF16)
            d = jnp.concatenate([d, jnp.zeros((16, wide - length), F32)], 1)
            after.append(pltpu.roll(totals[head], 16, 1) + d)
        return tuple(after)

    empty = jnp.zeros((16, wide), F32)
    totals = lax.fori_loop(0, tok // 16, step, (empty, empty))
    sub = lax.broadcasted_iota(jnp.int32, (16, wide), 0)
    for head in range(2):
        total = totals[head]
        for bit in (1, 2, 4, 8):
            total = jnp.where((sub & bit) == 0, pltpu.roll(total, bit, 1), total)
        diag_ref[0, head : head + 1, :] = jnp.sum(total, axis=0, keepdims=True)
    dq = join_pair(mm(ds_ref[...], k_ref[...]), size) * (1.0 / math.sqrt(size))
    dq_ref[...] = dq.astype(BF16)
    queries = split_pair(q_ref[...].astype(F32), size)
    dk = mm(queries.T.astype(BF16), ds_ref[...]).astype(BF16)
    dv = mm(grads.T.astype(BF16), p_ref[0]).astype(BF16)
    dkv_ref[0] = dk
    dkv_ref[1] = dv
    weights = mm(jnp.concatenate([dk, dv], 0), act_ref[...])
    parts = (mm(dq.T.astype(BF16), own_ref[...]), weights[:lanes], weights[lanes:])
    gain = jnp.zeros((1, act_ref.shape[1]), F32)
    for i, (found, turned) in enumerate(zip(parts, (wqt_ref, wkt_ref, wvt_ref))):
        grad_ref[i] = found.T.astype(BF16)
        gain = gain + jnp.sum(found * turned[...].astype(F32), axis=0, keepdims=True)

    @pl.when(pair == 0)
    def _():
        gain_ref[...] = gain

    @pl.when(pair > 0)
    def _():
        gain_ref[...] += gain


def attend_back(half, probs, grad_heads, heads, query, key, value, act_all, act, turned, ready):
    length, width = act_all.shape
    tok = query.shape[0]
    pairs = probs.shape[0] // 2
    wide = length + tok
    lanes = width // (2 * pairs)
    column = lambda rows: pl.BlockSpec((rows, lanes), lambda p, h: (0, p + h[0] * pairs))
    whole = lambda rows, cols: pl.BlockSpec((rows, cols), lambda p, h: (0, 0))
    row = pl.BlockSpec((lanes, width), lambda p, h: (p + h[0] * pairs, 0))
    return pl.pallas_call(
        attend_back_kernel,
        grid_spec=pltpu.PrefetchScalarGridSpec(
            num_scalar_prefetch=1,
            grid=(pairs,),
            in_specs=[
                pl.BlockSpec((1, 2 * tok, length), lambda p, h: (p + h[0] * pairs, 0, 0)),
                column(tok), column(tok), column(tok), column(length), column(length),
                whole(length, width), whole(tok, width),
                row, row, row, pl.BlockSpec(memory_space=pl.ANY),
            ],
            out_specs=[
                pl.BlockSpec((tok, lanes), lambda p, h: (0, p)),
                pl.BlockSpec((2, lanes, length), lambda p, h: (0, p, 0)),
                pl.BlockSpec((3, width, lanes), lambda p, h: (0, 0, p)),
                pl.BlockSpec((1, width), lambda p, h: (0, 0)),
                pl.BlockSpec((1, 2, wide), lambda p, h: (p, 0, 0)),
            ],
            scratch_shapes=[
                pltpu.VMEM((2 * tok, length), F32),
                pltpu.VMEM((2 * tok, length), BF16),
                pltpu.VMEM((2 * tok, lanes), F32),
            ],
        ),
        out_shape=[
            jax.ShapeDtypeStruct((tok, width // 2), BF16),
            jax.ShapeDtypeStruct((2, width // 2, length), BF16),
            jax.ShapeDtypeStruct((3, width, width // 2), BF16),
            jax.ShapeDtypeStruct((1, width), F32),
            jax.ShapeDtypeStruct((pairs, 2, wide), F32),
        ],
        compiler_params=pltpu.CompilerParams(vmem_limit_bytes=56 * MIB),
        cost_estimate=pl.CostEstimate(
            flops=4 * length * width * width + 8 * tok * length * width,
            bytes_accessed=8 * length * width + 2 * pairs * tok * length,
            transcendentals=0,
        ),
        name="attend_back",
    )(half, probs, grad_heads, heads, query, key, value, act_all, act, *turned, ready)


def spread_kernel(half_ref, wka_ref, wva_ref, a_ref, wkb_ref, wvb_ref, b_ref, *refs):
    out_ref = refs[-1]
    tok = out_ref.shape[2]
    found = mm(jnp.concatenate([wka_ref[...], wva_ref[...]], 1), jnp.concatenate([a_ref[0], a_ref[1]], 0))
    found += mm(jnp.concatenate([wkb_ref[...], wvb_ref[...]], 1), jnp.concatenate([b_ref[0], b_ref[1]], 0))
    found = found.astype(BF16)
    for i in range(out_ref.shape[0]):
        out_ref[i] = found[:, i * tok : (i + 1) * tok]


def spread(half, w_key, w_value, terms_a, terms_b, tok, ready):
    width = w_key.shape[0]
    length = terms_a.shape[2]
    cols = width // 2
    weight_a = pl.BlockSpec((width, cols), lambda c, h: (0, h[0]))
    weight_b = pl.BlockSpec((width, cols), lambda c, h: (0, 1 - h[0]))
    terms = pl.BlockSpec((2, cols, 2 * tok), lambda c, h: (0, 0, c))
    return pl.pallas_call(
        spread_kernel,
        grid_spec=pltpu.PrefetchScalarGridSpec(
            num_scalar_prefetch=1,
            grid=(length // (2 * tok),),
            in_specs=[weight_a, weight_a, terms, weight_b, weight_b, terms]
            + [pl.BlockSpec(memory_space=pl.ANY)] * len(ready),
            out_specs=pl.BlockSpec((2, width, tok), lambda c, h: (c, 0, 0)),
        ),
        out_shape=jax.ShapeDtypeStruct((length // tok, width, tok), BF16),
        compiler_params=pltpu.CompilerParams(vmem_limit_bytes=56 * MIB),
        cost_estimate=pl.CostEstimate(
            flops=4 * length * width * width, bytes_accessed=6 * length * width, transcendentals=0
        ),
        name="spread",
    )(half, w_key, w_value, terms_a, w_key, w_value, terms_b, *ready)


def merge_kernel(mine_ref, other_ref, mine_out_ref, other_out_ref, small_ref, out_ref):
    count = out_ref.shape[0]
    rows = mine_ref.shape[1] // count
    for c in range(count):
        here = slice(c * rows, (c + 1) * rows)
        for i in range(3):
            found = mine_ref[i, here, :].astype(F32) + other_ref[i, here, :].astype(F32)
            out_ref[c, i * rows : (i + 1) * rows, :] = found.astype(BF16)
        found = mine_out_ref[here, :].astype(F32) + other_out_ref[here, :].astype(F32)
        out_ref[c, 3 * rows : 4 * rows, :] = found.astype(BF16)
        out_ref[c, 4 * rows :, :] = small_ref[c]


def merge_halves(mine, other, mine_out, other_out, small):
    count, extra, cols = small.shape
    width = mine.shape[1]
    rows = width // count
    steps = 4
    each = count // steps
    triple = pl.BlockSpec((3, each * rows, cols), lambda c: (0, c, 0))
    single = pl.BlockSpec((each * rows, cols), lambda c: (c, 0))
    return pl.pallas_call(
        merge_kernel,
        grid=(steps,),
        in_specs=[triple, triple, single, single, pl.BlockSpec((each, extra, cols), lambda c: (c, 0, 0))],
        out_specs=pl.BlockSpec((each, 4 * rows + extra, cols), lambda c: (c, 0, 0)),
        out_shape=jax.ShapeDtypeStruct((count, 4 * rows + extra, cols), BF16),
        compiler_params=pltpu.CompilerParams(vmem_limit_bytes=56 * MIB),
        name="merge_halves",
    )(mine, other, mine_out, other_out, small)


def unpack_kernel(core_ref, mine_ref, other_ref, *out_refs):
    count = mine_ref.shape[0]
    rows, width = out_refs[0].shape
    rows = rows // count
    cols = width // 2
    low = core_ref[0] == 0
    for c in range(count):
        for i, out_ref in enumerate(out_refs):
            mine = mine_ref[c, i * rows : (i + 1) * rows, :].astype(F32)
            other = other_ref[c, i * rows : (i + 1) * rows, :].astype(F32)
            out_ref[c * rows : (c + 1) * rows, :cols] = jnp.where(low, mine, other)
            out_ref[c * rows : (c + 1) * rows, cols:] = jnp.where(low, other, mine)


def unpack_halves(core, mine, other):
    count, total, cols = mine.shape
    width = 2 * cols
    rows = width // count
    steps = 4
    each = count // steps
    block = pl.BlockSpec((each, total, cols), lambda c, core: (c, 0, 0))
    return pl.pallas_call(
        unpack_kernel,
        grid_spec=pltpu.PrefetchScalarGridSpec(
            num_scalar_prefetch=1,
            grid=(steps,),
            in_specs=[block, block],
            out_specs=[pl.BlockSpec((each * rows, width), lambda c, core: (c, 0))] * 4,
        ),
        out_shape=[jax.ShapeDtypeStruct((width, width), F32)] * 4,
        compiler_params=pltpu.CompilerParams(vmem_limit_bytes=56 * MIB),
        name="unpack_halves",
    )(core, mine, other)


def expert_kernel(rows_ref, win_ref, wout_ref, out_ref, total_ref):
    width = win_ref.shape[0]
    step = pl.program_id(0)
    sent = rows_ref[:, :width]
    grad = rows_ref[:, width:]
    hidden, slope = gelu_parts(mm(sent, win_ref[...]))
    grad_pre = (mm(grad, wout_ref[...], NT) * slope).astype(BF16)
    forward = mm(hidden.astype(BF16), wout_ref[...])
    backward = mm(grad_pre, win_ref[...], NT)

    @pl.when(step == 0)
    def _():
        total_ref[:, :width] = forward
        total_ref[:, width:] = backward

    @pl.when(step > 0)
    def _():
        total_ref[:, :width] += forward
        total_ref[:, width:] += backward

    @pl.when(step == pl.num_programs(0) - 1)
    def _():
        out_ref[...] = total_ref[...].astype(BF16)


def expert_both(rows, w_in, w_out):
    count, double = rows.shape
    width, units = w_in.shape
    chunk = 768 if units % 768 == 0 else units
    return pl.pallas_call(
        expert_kernel,
        grid=(units // chunk,),
        in_specs=[
            pl.BlockSpec((count, double), lambda c: (0, 0)),
            pl.BlockSpec((width, chunk), lambda c: (0, c)),
            pl.BlockSpec((chunk, width), lambda c: (c, 0)),
        ],
        out_specs=pl.BlockSpec((count, double), lambda c: (0, 0)),
        out_shape=jax.ShapeDtypeStruct((count, double), BF16),
        scratch_shapes=[pltpu.VMEM((count, double), F32)],
        compiler_params=pltpu.CompilerParams(vmem_limit_bytes=56 * MIB),
        cost_estimate=pl.CostEstimate(
            flops=8 * count * width * units, bytes_accessed=4 * width * units, transcendentals=count * units
        ),
        name="expert_both",
    )(rows, w_in, w_out)


def expert_grad_kernel(place_ref, *refs):
    row_refs, (wint_ref, wout_ref, out_ref, rows_ref) = refs[:-4], refs[-4:]
    width = wint_ref.shape[1]
    count = row_refs[0].shape[0]

    @pl.when(pl.program_id(0) == 0)
    def _():
        for i, ref in enumerate(row_refs):
            rows_ref[i * count : (i + 1) * count, :] = ref[...]

    sent = rows_ref[:, :width]
    grad = rows_ref[:, width:]
    hidden, slope = gelu_parts(mm(wint_ref[...], sent, NT))
    grad_pre = (mm(wout_ref[...], grad, NT) * slope).astype(BF16)
    found = (mm(grad_pre, sent).astype(BF16), mm(hidden.astype(BF16), grad).astype(BF16))
    share = out_ref.shape[3]
    for d in range(2):
        to = lax.rem(d + place_ref[1], 2)
        for i in range(2):
            out_ref[to, 0, i] = found[i][d * share : (d + 1) * share]


def expert_grads(place, parts, w_in_t, w_out, side):
    units, width = w_out.shape
    count = sum(part.shape[0] for part in parts)
    chunk = units // side
    weight = pl.BlockSpec((chunk, width), lambda c, place: (c, 0))
    return pl.pallas_call(
        expert_grad_kernel,
        grid_spec=pltpu.PrefetchScalarGridSpec(
            num_scalar_prefetch=1,
            grid=(side,),
            in_specs=[pl.BlockSpec(part.shape, lambda c, place: (0, 0)) for part in parts] + [weight, weight],
            out_specs=pl.BlockSpec(
                (2, 1, 2, chunk // 2, width),
                lambda c, place: (0, lax.rem(c + side - place[0], side), 0, 0, 0),
            ),
            scratch_shapes=[pltpu.VMEM((count, 2 * width), BF16)],
        ),
        out_shape=jax.ShapeDtypeStruct((2, side, 2, chunk // 2, width), BF16),
        compiler_params=pltpu.CompilerParams(vmem_limit_bytes=56 * MIB),
        cost_estimate=pl.CostEstimate(
            flops=8 * count * width * units, bytes_accessed=8 * width * units, transcendentals=count * units
        ),
        name="expert_grads",
    )(place, *parts, w_in_t, w_out)


def per_device(
    ctx_count,
    dp_count,
    inputs,
    cotangent,
    norm1_gain,
    w_query,
    w_key,
    w_value,
    w_output,
    bias_table,
    buckets,
    norm2_gain,
    w_router,
    routes,
    w_in,
    w_out,
):
    tok_count, width = inputs.shape[1:]
    length = (buckets.shape[0] + 1) // 2
    bucket_count, head_count = bias_table.shape
    expert_count = w_router.shape[1]
    capacity = (tok_count * 5 + 4 * expert_count - 1) // (4 * expert_count)
    side = math.isqrt(ctx_count)
    units = w_in.shape[2]
    context = lax.axis_index("context")
    ctx_y, ctx_x = context // side, context % side
    dp = lax.axis_index("dp")

    def ring(values, along_y, step):
        pairs = []
        for c in range(ctx_count):
            y, x = divmod(c, side)
            to = ((y + step) % side) * side + x if along_y else y * side + (x + step) % side
            pairs.append((c, to))
        return lax.ppermute(values, "context", pairs)

    inputs_f = inputs[0].astype(F32)
    gain1 = norm1_gain.astype(F32)
    scale1 = rms_stats(inputs_f)
    act = (inputs_f * scale1 * gain1).astype(BF16)
    act_all = lax.all_gather(act, "context", axis=0, tiled=True)

    padded = jnp.pad(buckets, (0, 1))
    start = length - tok_count - context * tok_count
    near = lax.dynamic_slice_in_dim(padded, start, length + tok_count)
    onehot = (jnp.arange(bucket_count, dtype=jnp.int32)[:, None] == near[None, :]).astype(BF16)
    window = lax.dot_general(bias_table, onehot, (((0,), (0,)), ((), ())), preferred_element_type=F32)
    window = window.reshape(head_count // 2, 2, length + tok_count)

    route = routes[0, :, 0]
    chosen = (route[:, None] == jnp.arange(expert_count, dtype=jnp.int32)[None, :]).astype(jnp.int32)
    chosen_f = chosen.astype(F32)
    slot_of = jnp.sum((jnp.cumsum(chosen, axis=0) - 1) * chosen, axis=-1)
    target = route * capacity + slot_of
    slots = jnp.arange(expert_count * capacity, dtype=jnp.int32)
    dispatch = (slots[:, None] == target[None, :]).astype(BF16)
    collect = (target[:, None] == slots[None, :]).astype(BF16)
    quarter = units // side
    w_in_slice = lax.dynamic_slice_in_dim(w_in[0], ctx_y * quarter, quarter, 1).T
    w_out_slice = lax.dynamic_slice_in_dim(w_out[0], ctx_y * quarter, quarter, 0)

    turned = (w_query.T, w_key.T, w_value.T)
    ready = (w_in_slice, w_out_slice) + turned
    query, key, value, heads_f, inverse, probs = attend(
        act_all, act, w_query, w_key, w_value, window, ready
    )
    heads_out = heads_f.astype(BF16)
    resid = inputs_f + mm(heads_out, w_output)
    gain2 = norm2_gain.astype(F32)
    scale2 = rms_stats(resid)
    normed2 = resid * scale2 * gain2
    router = w_router.astype(F32)
    logits = jnp.dot(normed2, router, precision=HIGHEST)
    router_exp = jnp.exp(logits - jnp.max(logits, axis=-1, keepdims=True))
    router_probs = router_exp / jnp.sum(router_exp, axis=-1, keepdims=True)
    gate = jnp.sum(router_probs * chosen_f, axis=-1)
    grad_out = cotangent[0].astype(F32)
    grad_picked = gate[:, None] * grad_out
    going = jnp.concatenate([normed2.astype(BF16), grad_picked.astype(BF16)], 1)
    going = mm(dispatch, going).astype(BF16).reshape(expert_count, capacity, 2 * width)
    arrived = lax.all_to_all(going, "expert", split_axis=0, concat_axis=0, tiled=True)
    arrived = arrived.reshape(expert_count * capacity, 2 * width)
    results = expert_both(arrived, w_in[0], w_out[0])
    results = results.reshape(expert_count, capacity, 2 * width)
    returned = lax.all_to_all(results, "expert", split_axis=0, concat_axis=0, tiled=True)
    returned = mm(collect, returned.reshape(expert_count * capacity, 2 * width))
    picked, grad_sent = returned[:, :width], returned[:, width:]
    mixed = resid + gate[:, None] * picked

    parts = [arrived] + [ring(arrived, True, step) for step in range(1, side)]
    shares = expert_grads(jnp.stack([ctx_x, dp]).astype(jnp.int32), parts, w_in_slice, w_out_slice, side)
    grad_gate = jnp.sum(grad_out * picked, axis=-1)
    grad_logits = (grad_gate * gate)[:, None] * (chosen_f - router_probs)
    grad_router = lax.dot_general(grad_logits, normed2, (((0,), (0,)), ((), ())), precision=HIGHEST)
    grad_normed2 = grad_sent + jnp.dot(grad_logits, router.T, precision=HIGHEST)
    grad_gain2 = jnp.sum(grad_normed2 * resid * scale2, axis=0)
    grad_resid = rms_back(grad_normed2, resid, scale2, gain2) + grad_out
    grad_attn = grad_resid.astype(BF16)
    grad_heads = mm(grad_attn, w_output, NT).astype(BF16)
    scaled = (grad_heads.astype(F32) * inverse).astype(BF16)

    expert = lax.axis_index("expert")
    core = (expert % 2)[None]
    swap = [(e, e ^ 1) for e in range(expert_count)]
    cols = width // 2
    both_out = []
    for half in (1 - core[0], core[0]):
        attn_half = lax.dynamic_slice_in_dim(grad_attn, half * cols, cols, 1)
        both_out.append(jnp.dot(heads_out.T, attn_half, preferred_element_type=F32).astype(BF16))
    other_out = lax.ppermute(both_out[0], "expert", swap)
    back = functools.partial(
        attend_back, probs=probs, grad_heads=scaled, heads=heads_f, query=query, key=key, value=value,
        act_all=act_all, act=act, turned=turned,
    )
    dq_a, terms_a, grads_a, gain_a, diag_a = back(1 - core, ready=arrived)
    other = lax.ppermute(grads_a, "expert", swap)
    dq_b, terms_b, grads_b, gain_b, diag_b = back(core, ready=shares)
    low = core[0] == 0
    in_order = lambda a, b, axis: jnp.concatenate([jnp.where(low, b, a), jnp.where(low, a, b)], axis)
    diagonals = in_order(diag_a, diag_b, 0)
    diagonals = diagonals.reshape(head_count, length + tok_count)
    grad_table = lax.dot_general(
        diagonals, onehot.astype(F32), (((1,), (1,)), ((), ())), precision=HIGHEST
    )
    small = jnp.concatenate(
        [(gain_a + gain_b)[0] / gain1, grad_gain2, grad_router.reshape(-1), grad_table.reshape(-1)]
    )
    small = jnp.pad(small, (0, ctx_count * 16 * cols - small.size)).astype(BF16)
    merged = merge_halves(grads_b, other, both_out[1], other_out, small.reshape(ctx_count, 16, cols))
    shares, merged = lax.optimization_barrier((shares, merged))
    other = lax.ppermute(shares[1], "dp", [(0, 1), (1, 0)])
    paired = (shares[0].astype(F32) + other.astype(F32)).astype(BF16)
    expert_sum = paired[0].astype(F32)
    for step in range(1, side):
        expert_sum = expert_sum + ring(paired[step], False, step).astype(F32)
    grad_w_in_out = expert_sum[0].T[None]
    grad_w_out_out = expert_sum[1][None]
    part = spread(core, w_key, w_value, terms_b, terms_a, tok_count, (expert_sum, merged))
    merged = lax.all_to_all(merged, "context", split_axis=0, concat_axis=0, tiled=True)
    merged = jnp.sum(merged.astype(F32), axis=0).astype(BF16)
    part, merged = lax.optimization_barrier((part, merged))
    total = merged.astype(F32)
    depth = expert_count // 2 * dp_count
    for step in range(1, depth):
        pairs = []
        for e in range(expert_count):
            for d in range(dp_count):
                z = (e // 2 * dp_count + d + step) % depth
                to = (z // dp_count * 2 + e % 2) * dp_count + z % dp_count
                pairs.append((e * dp_count + d, to))
        total = total + lax.ppermute(merged, ("expert", "dp"), pairs).astype(F32)
    whole = lax.all_gather(total.astype(BF16), "context", axis=0)
    other = lax.ppermute(whole, "expert", swap)
    grad_w_query, grad_w_key, grad_w_value, grad_w_output = unpack_halves(core, whole, other)
    rows = 4 * width // ctx_count
    small = (whole[:, rows:].astype(F32) + other[:, rows:].astype(F32)).reshape(-1)
    edges = [width, 2 * width, (2 + expert_count) * width, (2 + expert_count) * width + bucket_count * head_count]
    grad_gain1, grad_gain2, grad_router, grad_table = jnp.split(small[: edges[3]], edges[:3])
    grad_router = grad_router.reshape(expert_count, width).T
    grad_table = grad_table.reshape(head_count, bucket_count).T
    grad_query = in_order(dq_a, dq_b, 1)

    part = lax.all_to_all(part, "context", split_axis=0, concat_axis=0, tiled=True)
    grad_act = mm(grad_query, w_query, NT) + jnp.sum(part.astype(F32), axis=0).T
    grad_inputs = rms_back(grad_act, inputs_f, scale1, gain1) + grad_resid
    return (
        mixed[None].astype(BF16),
        grad_inputs[None].astype(BF16),
        grad_gain1,
        grad_w_query,
        grad_w_key,
        grad_w_value,
        grad_w_output,
        grad_table,
        grad_gain2,
        grad_router,
        grad_w_in_out,
        grad_w_out_out,
    )


def solution(mesh):
    tokens = P(("expert", "dp"), "context", None)
    return jax.shard_map(
        functools.partial(per_device, mesh.shape["context"], mesh.shape["dp"]),
        mesh=mesh,
        in_specs=(
            tokens, tokens, P(), P(), P(), P(), P(), P(), P(), P(), P(), tokens,
            P("expert", None, None), P("expert", None, None),
        ),
        out_specs=(
            tokens, tokens, P(), P(), P(), P(), P(), P(), P(), P(),
            P("expert", None, ("context", "dp")), P("expert", ("context", "dp"), None),
        ),
        check_vma=False,
    )
```

```python
import functools
import math

import jax
import jax.numpy as jnp
from jax import lax
from jax.experimental import pallas as pl
from jax.experimental.pallas import tpu as pltpu
from jax.sharding import PartitionSpec as P

EPS = 1e-06
F32 = jnp.float32
BF16 = jnp.bfloat16
NN = (((1,), (0,)), ((), ()))
NT = (((1,), (1,)), ((), ()))
HIGHEST = lax.Precision.HIGHEST
MIB = 1 << 20


def mm(left, right, dims=NN):
    return lax.dot_general(left, right, dims, preferred_element_type=F32)


def rms_stats(values):
    return lax.rsqrt(jnp.mean(values * values, axis=-1, keepdims=True) + EPS)


def rms_back(grad, values, scale, gain):
    weighted = grad * gain
    inner = jnp.mean(weighted * values, axis=-1, keepdims=True)
    return scale * weighted - values * (scale * scale * scale * inner)


def gelu_parts(u):
    c = math.sqrt(2.0 / math.pi)
    sq = u * u
    t = jnp.tanh(c * u * (1.0 + 0.044715 * sq))
    half = 0.5 * (1.0 + t)
    slope = half + (0.5 * c) * u * (1.0 - t * t) * (1.0 + (3 * 0.044715) * sq)
    return u * half, slope


def first_half(shape, size):
    return lax.broadcasted_iota(jnp.int32, shape, 1) < size


def split_pair(pair, size):
    first = first_half(pair.shape, size)
    zero = jnp.zeros_like(pair)
    return jnp.concatenate([jnp.where(first, pair, zero), jnp.where(first, zero, pair)], 0)


def join_pair(stacked, size):
    rows = stacked.shape[0] // 2
    return jnp.where(first_half((rows, 2 * size), size), stacked[:rows], stacked[rows:])


def attend_kernel(act_ref, own_ref, wq_ref, wk_ref, wv_ref, win_ref, *refs):
    q_ref, k_ref, v_ref, o_ref, inv_ref, p_ref, s_ref, m_ref, ext_ref = refs[-9:]
    tok = own_ref.shape[0]
    length = act_ref.shape[0]
    wide = win_ref.shape[2]
    lanes = wq_ref.shape[1]
    size = lanes // 2
    query = mm(own_ref[...], wq_ref[...]).astype(BF16)
    query = query.astype(F32) * (1.0 / math.sqrt(size))
    q_ref[...] = query.astype(BF16)
    both = mm(act_ref[...], jnp.concatenate([wk_ref[...], wv_ref[...]], 1)).astype(BF16)
    k_ref[...] = both[:, :lanes]
    v_ref[...] = both[:, lanes:]
    ext_ref[:, :lanes] = both[:, lanes:]
    ext_ref[:, lanes:] = jnp.ones((length, lanes), BF16)
    s_ref[...] = mm(split_pair(query, size).astype(BF16), k_ref[...], NT)
    sub = lax.broadcasted_iota(jnp.int32, (16, wide), 0)

    def first_band(head):
        band = jnp.broadcast_to(win_ref[0, head : head + 1, :], (16, wide))
        band = pltpu.roll(band, wide - (tok - 1), 1)
        for bit in (1, 2, 4, 8):
            band = jnp.where((sub & bit) != 0, pltpu.roll(band, bit, 1), band)
        return band

    def rows_of(head, r):
        return pl.ds(pl.multiple_of(head * tok + r * 16, 16), 16)

    def add_bias(r, bands):
        for head in range(2):
            rows = rows_of(head, r)
            s = s_ref[rows, :] + bands[head][:, :length]
            s_ref[rows, :] = s
            tops = [s[:, c : c + lanes] for c in range(0, length, lanes)]
            while len(tops) > 1:
                tops = [jnp.maximum(a, b) for a, b in zip(tops[::2], tops[1::2])]
            m_ref[rows, :] = tops[0]
        return tuple(pltpu.roll(band, 16, 1) for band in bands)

    def exponents(r, carry):
        for part in range(4):
            rows = rows_of(0, 4 * r + part)
            top = jnp.concatenate([m_ref[rows, :]] * (length // lanes), 1)
            p_ref[0, rows, :] = jnp.exp(s_ref[rows, :] - top).astype(BF16)
        return carry

    lax.fori_loop(0, tok // 16, add_bias, (first_band(0), first_band(1)))
    m_ref[...] = jnp.broadcast_to(jnp.max(m_ref[...], axis=1, keepdims=True), m_ref.shape)
    lax.fori_loop(0, tok // 32, exponents, 0)
    summed = mm(p_ref[0], ext_ref[...])
    inverse = 1.0 / join_pair(summed[:, lanes:], size)
    inv_ref[...] = inverse
    o_ref[...] = join_pair(summed[:, :lanes], size) * inverse


def attend(act_all, act, w_query, w_key, w_value, window, ready):
    length, width = act_all.shape
    tok = act.shape[0]
    pairs, _, wide = window.shape
    lanes = width // pairs
    column = lambda rows: pl.BlockSpec((rows, lanes), lambda p: (0, p))
    whole = lambda rows: pl.BlockSpec((rows, width), lambda p: (0, 0))
    return pl.pallas_call(
        attend_kernel,
        grid=(pairs,),
        in_specs=[
            whole(length), whole(tok), column(width), column(width), column(width),
            pl.BlockSpec((1, 2, wide), lambda p: (p, 0, 0)),
        ] + [pl.BlockSpec(memory_space=pl.ANY)] * len(ready),
        out_specs=[
            column(tok), column(length), column(length), column(tok), column(tok),
            pl.BlockSpec((1, 2 * tok, length), lambda p: (p, 0, 0)),
        ],
        out_shape=[
            jax.ShapeDtypeStruct((tok, width), BF16),
            jax.ShapeDtypeStruct((length, width), BF16),
            jax.ShapeDtypeStruct((length, width), BF16),
            jax.ShapeDtypeStruct((tok, width), F32),
            jax.ShapeDtypeStruct((tok, width), F32),
            jax.ShapeDtypeStruct((pairs, 2 * tok, length), BF16),
        ],
        scratch_shapes=[
            pltpu.VMEM((2 * tok, length), F32),
            pltpu.VMEM((2 * tok, lanes), F32),
            pltpu.VMEM((length, 2 * lanes), BF16),
        ],
        compiler_params=pltpu.CompilerParams(vmem_limit_bytes=56 * MIB),
        cost_estimate=pl.CostEstimate(
            flops=4 * length * width * width + 8 * tok * length * width,
            bytes_accessed=12 * length * width + 4 * pairs * tok * length,
            transcendentals=2 * pairs * tok * length,
        ),
        name="attend",
    )(act_all, act, w_query, w_key, w_value, window, *ready)


def attend_back_kernel(half_ref, p_ref, do_ref, o_ref, q_ref, k_ref, v_ref, act_ref, own_ref,
                       wqt_ref, wkt_ref, wvt_ref, ready_ref,
                       dq_ref, dkv_ref, grad_ref, gain_ref, diag_ref,
                       dp_ref, ds_ref, delta_ref):
    tok = do_ref.shape[0]
    length = act_ref.shape[0]
    lanes = q_ref.shape[1]
    wide = diag_ref.shape[2]
    size = lanes // 2
    pair = pl.program_id(0)
    grad = do_ref[...].astype(F32)
    grads = split_pair(grad, size)
    delta = jnp.sum(split_pair(grad * o_ref[...], size), axis=1, keepdims=True)
    delta_ref[...] = jnp.broadcast_to(delta, delta_ref.shape)
    dp_ref[...] = mm(grads.astype(BF16), v_ref[...], NT)

    def step(r, totals):
        after = []
        for head in range(2):
            rows = pl.ds(pl.multiple_of(head * tok + r * 16, 16), 16)
            less = jnp.concatenate([delta_ref[rows, :]] * (length // lanes), 1)
            d = p_ref[0, rows, :].astype(F32) * (dp_ref[rows, :] - less)
            ds_ref[rows, :] = d.astype(BF16)
            d = jnp.concatenate([d, jnp.zeros((16, wide - length), F32)], 1)
            after.append(pltpu.roll(totals[head], 16, 1) + d)
        return tuple(after)

    empty = jnp.zeros((16, wide), F32)
    totals = lax.fori_loop(0, tok // 16, step, (empty, empty))
    sub = lax.broadcasted_iota(jnp.int32, (16, wide), 0)
    for head in range(2):
        total = totals[head]
        for bit in (1, 2, 4, 8):
            total = jnp.where((sub & bit) == 0, pltpu.roll(total, bit, 1), total)
        diag_ref[0, head : head + 1, :] = jnp.sum(total, axis=0, keepdims=True)
    dq = join_pair(mm(ds_ref[...], k_ref[...]), size) * (1.0 / math.sqrt(size))
    dq_ref[...] = dq.astype(BF16)
    queries = split_pair(q_ref[...].astype(F32), size)
    dk = mm(queries.T.astype(BF16), ds_ref[...]).astype(BF16)
    dv = mm(grads.T.astype(BF16), p_ref[0]).astype(BF16)
    dkv_ref[0] = dk
    dkv_ref[1] = dv
    weights = mm(jnp.concatenate([dk, dv], 0), act_ref[...])
    parts = (mm(dq.T.astype(BF16), own_ref[...]), weights[:lanes], weights[lanes:])
    gain = jnp.zeros((1, act_ref.shape[1]), F32)
    for i, (found, turned) in enumerate(zip(parts, (wqt_ref, wkt_ref, wvt_ref))):
        grad_ref[i] = found.T.astype(BF16)
        gain = gain + jnp.sum(found * turned[...].astype(F32), axis=0, keepdims=True)

    @pl.when(pair == 0)
    def _():
        gain_ref[...] = gain

    @pl.when(pair > 0)
    def _():
        gain_ref[...] += gain


def attend_back(half, probs, grad_heads, heads, query, key, value, act_all, act, turned, ready):
    length, width = act_all.shape
    tok = query.shape[0]
    pairs = probs.shape[0] // 2
    wide = length + tok
    lanes = width // (2 * pairs)
    column = lambda rows: pl.BlockSpec((rows, lanes), lambda p, h: (0, p + h[0] * pairs))
    whole = lambda rows, cols: pl.BlockSpec((rows, cols), lambda p, h: (0, 0))
    row = pl.BlockSpec((lanes, width), lambda p, h: (p + h[0] * pairs, 0))
    return pl.pallas_call(
        attend_back_kernel,
        grid_spec=pltpu.PrefetchScalarGridSpec(
            num_scalar_prefetch=1,
            grid=(pairs,),
            in_specs=[
                pl.BlockSpec((1, 2 * tok, length), lambda p, h: (p + h[0] * pairs, 0, 0)),
                column(tok), column(tok), column(tok), column(length), column(length),
                whole(length, width), whole(tok, width),
                row, row, row, pl.BlockSpec(memory_space=pl.ANY),
            ],
            out_specs=[
                pl.BlockSpec((tok, lanes), lambda p, h: (0, p)),
                pl.BlockSpec((2, lanes, length), lambda p, h: (0, p, 0)),
                pl.BlockSpec((3, width, lanes), lambda p, h: (0, 0, p)),
                pl.BlockSpec((1, width), lambda p, h: (0, 0)),
                pl.BlockSpec((1, 2, wide), lambda p, h: (p, 0, 0)),
            ],
            scratch_shapes=[
                pltpu.VMEM((2 * tok, length), F32),
                pltpu.VMEM((2 * tok, length), BF16),
                pltpu.VMEM((2 * tok, lanes), F32),
            ],
        ),
        out_shape=[
            jax.ShapeDtypeStruct((tok, width // 2), BF16),
            jax.ShapeDtypeStruct((2, width // 2, length), BF16),
            jax.ShapeDtypeStruct((3, width, width // 2), BF16),
            jax.ShapeDtypeStruct((1, width), F32),
            jax.ShapeDtypeStruct((pairs, 2, wide), F32),
        ],
        compiler_params=pltpu.CompilerParams(vmem_limit_bytes=56 * MIB),
        cost_estimate=pl.CostEstimate(
            flops=4 * length * width * width + 8 * tok * length * width,
            bytes_accessed=8 * length * width + 2 * pairs * tok * length,
            transcendentals=0,
        ),
        name="attend_back",
    )(half, probs, grad_heads, heads, query, key, value, act_all, act, *turned, ready)


def spread_kernel(half_ref, wka_ref, wva_ref, a_ref, wkb_ref, wvb_ref, b_ref, *refs):
    out_ref = refs[-1]
    tok = out_ref.shape[2]
    found = mm(jnp.concatenate([wka_ref[...], wva_ref[...]], 1), jnp.concatenate([a_ref[0], a_ref[1]], 0))
    found += mm(jnp.concatenate([wkb_ref[...], wvb_ref[...]], 1), jnp.concatenate([b_ref[0], b_ref[1]], 0))
    found = found.astype(BF16)
    for i in range(out_ref.shape[0]):
        out_ref[i] = found[:, i * tok : (i + 1) * tok]


def spread(half, w_key, w_value, terms_a, terms_b, tok, ready):
    width = w_key.shape[0]
    length = terms_a.shape[2]
    cols = width // 2
    weight_a = pl.BlockSpec((width, cols), lambda c, h: (0, h[0]))
    weight_b = pl.BlockSpec((width, cols), lambda c, h: (0, 1 - h[0]))
    terms = pl.BlockSpec((2, cols, 2 * tok), lambda c, h: (0, 0, c))
    return pl.pallas_call(
        spread_kernel,
        grid_spec=pltpu.PrefetchScalarGridSpec(
            num_scalar_prefetch=1,
            grid=(length // (2 * tok),),
            in_specs=[weight_a, weight_a, terms, weight_b, weight_b, terms]
            + [pl.BlockSpec(memory_space=pl.ANY)] * len(ready),
            out_specs=pl.BlockSpec((2, width, tok), lambda c, h: (c, 0, 0)),
        ),
        out_shape=jax.ShapeDtypeStruct((length // tok, width, tok), BF16),
        compiler_params=pltpu.CompilerParams(vmem_limit_bytes=56 * MIB),
        cost_estimate=pl.CostEstimate(
            flops=4 * length * width * width, bytes_accessed=6 * length * width, transcendentals=0
        ),
        name="spread",
    )(half, w_key, w_value, terms_a, w_key, w_value, terms_b, *ready)


def merge_kernel(mine_ref, other_ref, mine_out_ref, other_out_ref, small_ref, out_ref):
    count = out_ref.shape[0]
    rows = mine_ref.shape[1] // count
    for c in range(count):
        here = slice(c * rows, (c + 1) * rows)
        for i in range(3):
            found = mine_ref[i, here, :].astype(F32) + other_ref[i, here, :].astype(F32)
            out_ref[c, i * rows : (i + 1) * rows, :] = found.astype(BF16)
        found = mine_out_ref[here, :].astype(F32) + other_out_ref[here, :].astype(F32)
        out_ref[c, 3 * rows : 4 * rows, :] = found.astype(BF16)
        out_ref[c, 4 * rows :, :] = small_ref[c]


def merge_halves(mine, other, mine_out, other_out, small):
    count, extra, cols = small.shape
    width = mine.shape[1]
    rows = width // count
    steps = 4
    each = count // steps
    triple = pl.BlockSpec((3, each * rows, cols), lambda c: (0, c, 0))
    single = pl.BlockSpec((each * rows, cols), lambda c: (c, 0))
    return pl.pallas_call(
        merge_kernel,
        grid=(steps,),
        in_specs=[triple, triple, single, single, pl.BlockSpec((each, extra, cols), lambda c: (c, 0, 0))],
        out_specs=pl.BlockSpec((each, 4 * rows + extra, cols), lambda c: (c, 0, 0)),
        out_shape=jax.ShapeDtypeStruct((count, 4 * rows + extra, cols), BF16),
        compiler_params=pltpu.CompilerParams(vmem_limit_bytes=56 * MIB),
        name="merge_halves",
    )(mine, other, mine_out, other_out, small)


def unpack_kernel(core_ref, mine_ref, other_ref, *out_refs):
    count = mine_ref.shape[0]
    rows, width = out_refs[0].shape
    rows = rows // count
    cols = width // 2
    low = core_ref[0] == 0
    for c in range(count):
        for i, out_ref in enumerate(out_refs):
            mine = mine_ref[c, i * rows : (i + 1) * rows, :].astype(F32)
            other = other_ref[c, i * rows : (i + 1) * rows, :].astype(F32)
            out_ref[c * rows : (c + 1) * rows, :cols] = jnp.where(low, mine, other)
            out_ref[c * rows : (c + 1) * rows, cols:] = jnp.where(low, other, mine)


def unpack_halves(core, mine, other):
    count, total, cols = mine.shape
    width = 2 * cols
    rows = width // count
    steps = 4
    each = count // steps
    block = pl.BlockSpec((each, total, cols), lambda c, core: (c, 0, 0))
    return pl.pallas_call(
        unpack_kernel,
        grid_spec=pltpu.PrefetchScalarGridSpec(
            num_scalar_prefetch=1,
            grid=(steps,),
            in_specs=[block, block],
            out_specs=[pl.BlockSpec((each * rows, width), lambda c, core: (c, 0))] * 4,
        ),
        out_shape=[jax.ShapeDtypeStruct((width, width), F32)] * 4,
        compiler_params=pltpu.CompilerParams(vmem_limit_bytes=56 * MIB),
        name="unpack_halves",
    )(core, mine, other)


def expert_kernel(rows_ref, win_ref, wout_ref, out_ref, total_ref):
    width = win_ref.shape[0]
    step = pl.program_id(0)
    sent = rows_ref[:, :width]
    grad = rows_ref[:, width:]
    hidden, slope = gelu_parts(mm(sent, win_ref[...]))
    grad_pre = (mm(grad, wout_ref[...], NT) * slope).astype(BF16)
    forward = mm(hidden.astype(BF16), wout_ref[...])
    backward = mm(grad_pre, win_ref[...], NT)

    @pl.when(step == 0)
    def _():
        total_ref[:, :width] = forward
        total_ref[:, width:] = backward

    @pl.when(step > 0)
    def _():
        total_ref[:, :width] += forward
        total_ref[:, width:] += backward

    @pl.when(step == pl.num_programs(0) - 1)
    def _():
        out_ref[...] = total_ref[...].astype(BF16)


def expert_both(rows, w_in, w_out):
    count, double = rows.shape
    width, units = w_in.shape
    chunk = 768 if units % 768 == 0 else units
    return pl.pallas_call(
        expert_kernel,
        grid=(units // chunk,),
        in_specs=[
            pl.BlockSpec((count, double), lambda c: (0, 0)),
            pl.BlockSpec((width, chunk), lambda c: (0, c)),
            pl.BlockSpec((chunk, width), lambda c: (c, 0)),
        ],
        out_specs=pl.BlockSpec((count, double), lambda c: (0, 0)),
        out_shape=jax.ShapeDtypeStruct((count, double), BF16),
        scratch_shapes=[pltpu.VMEM((count, double), F32)],
        compiler_params=pltpu.CompilerParams(vmem_limit_bytes=56 * MIB),
        cost_estimate=pl.CostEstimate(
            flops=8 * count * width * units, bytes_accessed=4 * width * units, transcendentals=count * units
        ),
        name="expert_both",
    )(rows, w_in, w_out)


def expert_grad_kernel(place_ref, *refs):
    row_refs, (wint_ref, wout_ref, out_ref, rows_ref) = refs[:-4], refs[-4:]
    width = wint_ref.shape[1]
    count = row_refs[0].shape[0]

    @pl.when(pl.program_id(0) == 0)
    def _():
        for i, ref in enumerate(row_refs):
            rows_ref[i * count : (i + 1) * count, :] = ref[...]

    sent = rows_ref[:, :width]
    grad = rows_ref[:, width:]
    hidden, slope = gelu_parts(mm(wint_ref[...], sent, NT))
    grad_pre = (mm(wout_ref[...], grad, NT) * slope).astype(BF16)
    found = (mm(grad_pre, sent).astype(BF16), mm(hidden.astype(BF16), grad).astype(BF16))
    share = out_ref.shape[3]
    for d in range(2):
        to = lax.rem(d + place_ref[1], 2)
        for i in range(2):
            out_ref[to, 0, i] = found[i][d * share : (d + 1) * share]


def expert_grads(place, parts, w_in_t, w_out, side):
    units, width = w_out.shape
    count = sum(part.shape[0] for part in parts)
    chunk = units // side
    weight = pl.BlockSpec((chunk, width), lambda c, place: (c, 0))
    return pl.pallas_call(
        expert_grad_kernel,
        grid_spec=pltpu.PrefetchScalarGridSpec(
            num_scalar_prefetch=1,
            grid=(side,),
            in_specs=[pl.BlockSpec(part.shape, lambda c, place: (0, 0)) for part in parts] + [weight, weight],
            out_specs=pl.BlockSpec(
                (2, 1, 2, chunk // 2, width),
                lambda c, place: (0, lax.rem(c + side - place[0], side), 0, 0, 0),
            ),
            scratch_shapes=[pltpu.VMEM((count, 2 * width), BF16)],
        ),
        out_shape=jax.ShapeDtypeStruct((2, side, 2, chunk // 2, width), BF16),
        compiler_params=pltpu.CompilerParams(vmem_limit_bytes=56 * MIB),
        cost_estimate=pl.CostEstimate(
            flops=8 * count * width * units, bytes_accessed=8 * width * units, transcendentals=count * units
        ),
        name="expert_grads",
    )(place, *parts, w_in_t, w_out)


def per_device(
    ctx_count,
    dp_count,
    inputs,
    cotangent,
    norm1_gain,
    w_query,
    w_key,
    w_value,
    w_output,
    bias_table,
    buckets,
    norm2_gain,
    w_router,
    routes,
    w_in,
    w_out,
):
    tok_count, width = inputs.shape[1:]
    length = (buckets.shape[0] + 1) // 2
    bucket_count, head_count = bias_table.shape
    expert_count = w_router.shape[1]
    capacity = (tok_count * 5 + 4 * expert_count - 1) // (4 * expert_count)
    side = math.isqrt(ctx_count)
    units = w_in.shape[2]
    context = lax.axis_index("context")
    ctx_y, ctx_x = context // side, context % side
    dp = lax.axis_index("dp")

    def ring(values, along_y, step):
        pairs = []
        for c in range(ctx_count):
            y, x = divmod(c, side)
            to = ((y + step) % side) * side + x if along_y else y * side + (x + step) % side
            pairs.append((c, to))
        return lax.ppermute(values, "context", pairs)

    inputs_f = inputs[0].astype(F32)
    gain1 = norm1_gain.astype(F32)
    scale1 = rms_stats(inputs_f)
    act = (inputs_f * scale1 * gain1).astype(BF16)
    act_all = lax.all_gather(act, "context", axis=0, tiled=True)

    padded = jnp.pad(buckets, (0, 1))
    start = length - tok_count - context * tok_count
    near = lax.dynamic_slice_in_dim(padded, start, length + tok_count)
    onehot = (jnp.arange(bucket_count, dtype=jnp.int32)[:, None] == near[None, :]).astype(BF16)
    window = lax.dot_general(bias_table, onehot, (((0,), (0,)), ((), ())), preferred_element_type=F32)
    window = window.reshape(head_count // 2, 2, length + tok_count)

    route = routes[0, :, 0]
    chosen = (route[:, None] == jnp.arange(expert_count, dtype=jnp.int32)[None, :]).astype(jnp.int32)
    chosen_f = chosen.astype(F32)
    slot_of = jnp.sum((jnp.cumsum(chosen, axis=0) - 1) * chosen, axis=-1)
    target = route * capacity + slot_of
    slots = jnp.arange(expert_count * capacity, dtype=jnp.int32)
    dispatch = (slots[:, None] == target[None, :]).astype(BF16)
    collect = (target[:, None] == slots[None, :]).astype(BF16)
    quarter = units // side
    w_in_slice = lax.dynamic_slice_in_dim(w_in[0], ctx_y * quarter, quarter, 1).T
    w_out_slice = lax.dynamic_slice_in_dim(w_out[0], ctx_y * quarter, quarter, 0)

    turned = (w_query.T, w_key.T, w_value.T)
    ready = (w_in_slice, w_out_slice) + turned
    query, key, value, heads_f, inverse, probs = attend(
        act_all, act, w_query, w_key, w_value, window, ready
    )
    heads_out = heads_f.astype(BF16)
    resid = inputs_f + mm(heads_out, w_output)
    gain2 = norm2_gain.astype(F32)
    scale2 = rms_stats(resid)
    normed2 = resid * scale2 * gain2
    router = w_router.astype(F32)
    logits = jnp.dot(normed2, router, precision=HIGHEST)
    router_exp = jnp.exp(logits - jnp.max(logits, axis=-1, keepdims=True))
    router_probs = router_exp / jnp.sum(router_exp, axis=-1, keepdims=True)
    gate = jnp.sum(router_probs * chosen_f, axis=-1)
    grad_out = cotangent[0].astype(F32)
    grad_picked = gate[:, None] * grad_out
    going = jnp.concatenate([normed2.astype(BF16), grad_picked.astype(BF16)], 1)
    going = mm(dispatch, going).astype(BF16).reshape(expert_count, capacity, 2 * width)
    arrived = lax.all_to_all(going, "expert", split_axis=0, concat_axis=0, tiled=True)
    arrived = arrived.reshape(expert_count * capacity, 2 * width)
    results = expert_both(arrived, w_in[0], w_out[0])
    results = results.reshape(expert_count, capacity, 2 * width)
    returned = lax.all_to_all(results, "expert", split_axis=0, concat_axis=0, tiled=True)
    returned = mm(collect, returned.reshape(expert_count * capacity, 2 * width))
    picked, grad_sent = returned[:, :width], returned[:, width:]
    mixed = resid + gate[:, None] * picked

    parts = [arrived] + [ring(arrived, True, step) for step in range(1, side)]
    shares = expert_grads(jnp.stack([ctx_x, dp]).astype(jnp.int32), parts, w_in_slice, w_out_slice, side)
    grad_gate = jnp.sum(grad_out * picked, axis=-1)
    grad_logits = (grad_gate * gate)[:, None] * (chosen_f - router_probs)
    grad_router = lax.dot_general(grad_logits, normed2, (((0,), (0,)), ((), ())), precision=HIGHEST)
    grad_normed2 = grad_sent + jnp.dot(grad_logits, router.T, precision=HIGHEST)
    grad_gain2 = jnp.sum(grad_normed2 * resid * scale2, axis=0)
    grad_resid = rms_back(grad_normed2, resid, scale2, gain2) + grad_out
    grad_attn = grad_resid.astype(BF16)
    grad_heads = mm(grad_attn, w_output, NT).astype(BF16)
    scaled = (grad_heads.astype(F32) * inverse).astype(BF16)

    expert = lax.axis_index("expert")
    core = (expert % 2)[None]
    swap = [(e, e ^ 1) for e in range(expert_count)]
    cols = width // 2
    both_out = []
    for half in (1 - core[0], core[0]):
        attn_half = lax.dynamic_slice_in_dim(grad_attn, half * cols, cols, 1)
        both_out.append(jnp.dot(heads_out.T, attn_half, preferred_element_type=F32).astype(BF16))
    other_out = lax.ppermute(both_out[0], "expert", swap)
    back = functools.partial(
        attend_back, probs=probs, grad_heads=scaled, heads=heads_f, query=query, key=key, value=value,
        act_all=act_all, act=act, turned=turned,
    )
    dq_a, terms_a, grads_a, gain_a, diag_a = back(1 - core, ready=arrived)
    other = lax.ppermute(grads_a, "expert", swap)
    dq_b, terms_b, grads_b, gain_b, diag_b = back(core, ready=shares)
    low = core[0] == 0
    in_order = lambda a, b, axis: jnp.concatenate([jnp.where(low, b, a), jnp.where(low, a, b)], axis)
    diagonals = in_order(diag_a, diag_b, 0)
    diagonals = diagonals.reshape(head_count, length + tok_count)
    grad_table = lax.dot_general(
        diagonals, onehot.astype(F32), (((1,), (1,)), ((), ())), precision=HIGHEST
    )
    small = jnp.concatenate(
        [(gain_a + gain_b)[0] / gain1, grad_gain2, grad_router.reshape(-1), grad_table.reshape(-1)]
    )
    small = jnp.pad(small, (0, ctx_count * 16 * cols - small.size)).astype(BF16)
    merged = merge_halves(grads_b, other, both_out[1], other_out, small.reshape(ctx_count, 16, cols))
    shares, merged = lax.optimization_barrier((shares, merged))
    other = lax.ppermute(shares[1], "dp", [(0, 1), (1, 0)])
    paired = (shares[0].astype(F32) + other.astype(F32)).astype(BF16)
    expert_sum = paired[0].astype(F32)
    for step in range(1, side):
        expert_sum = expert_sum + ring(paired[step], False, step).astype(F32)
    part = spread(core, w_key, w_value, terms_b, terms_a, tok_count, (merged,))
    merged = lax.all_to_all(merged, "context", split_axis=0, concat_axis=0, tiled=True)
    merged = jnp.sum(merged.astype(F32), axis=0).astype(BF16)
    part, merged, expert_sum = lax.optimization_barrier((part, merged, expert_sum))
    grad_w_in_out = expert_sum[0].T[None]
    grad_w_out_out = expert_sum[1][None]
    total = merged.astype(F32)
    depth = expert_count // 2 * dp_count
    for step in range(1, depth):
        pairs = []
        for e in range(expert_count):
            for d in range(dp_count):
                z = (e // 2 * dp_count + d + step) % depth
                to = (z // dp_count * 2 + e % 2) * dp_count + z % dp_count
                pairs.append((e * dp_count + d, to))
        total = total + lax.ppermute(merged, ("expert", "dp"), pairs).astype(F32)
    whole = lax.all_gather(total.astype(BF16), "context", axis=0)
    other = lax.ppermute(whole, "expert", swap)
    grad_w_query, grad_w_key, grad_w_value, grad_w_output = unpack_halves(core, whole, other)
    rows = 4 * width // ctx_count
    small = (whole[:, rows:].astype(F32) + other[:, rows:].astype(F32)).reshape(-1)
    edges = [width, 2 * width, (2 + expert_count) * width, (2 + expert_count) * width + bucket_count * head_count]
    grad_gain1, grad_gain2, grad_router, grad_table = jnp.split(small[: edges[3]], edges[:3])
    grad_router = grad_router.reshape(expert_count, width).T
    grad_table = grad_table.reshape(head_count, bucket_count).T
    grad_query = in_order(dq_a, dq_b, 1)

    part = lax.all_to_all(part, "context", split_axis=0, concat_axis=0, tiled=True)
    grad_act = mm(grad_query, w_query, NT) + jnp.sum(part.astype(F32), axis=0).T
    grad_inputs = rms_back(grad_act, inputs_f, scale1, gain1) + grad_resid
    return (
        mixed[None].astype(BF16),
        grad_inputs[None].astype(BF16),
        grad_gain1,
        grad_w_query,
        grad_w_key,
        grad_w_value,
        grad_w_output,
        grad_table,
        grad_gain2,
        grad_router,
        grad_w_in_out,
        grad_w_out_out,
    )


def solution(mesh):
    tokens = P(("expert", "dp"), "context", None)
    return jax.shard_map(
        functools.partial(per_device, mesh.shape["context"], mesh.shape["dp"]),
        mesh=mesh,
        in_specs=(
            tokens, tokens, P(), P(), P(), P(), P(), P(), P(), P(), P(), tokens,
            P("expert", None, None), P("expert", None, None),
        ),
        out_specs=(
            tokens, tokens, P(), P(), P(), P(), P(), P(), P(), P(),
            P("expert", None, ("context", "dp")), P("expert", ("context", "dp"), None),
        ),
        check_vma=False,
    )
```
